32 devices in a mesh: run: 2 (over y), gy: 4 (over z), gx: 2 (over x), gz: 2 (over core).
Axes of the slice: x: 2, y: 2, z: 4, core: 2. Of those that a mesh axis runs over, the one named last changes fastest.
Arguments:
- facies: int32 [64, 128, 256], P(('run', 'gx'), 'gy', 'gz'), parts along dimension 0, may hold values from 0 to 4
- pressure_old: float32 [64, 128, 256], P(('run', 'gx'), 'gy', 'gz'), parts along dimension 0, may hold values from -6 to 6
- saturation: float32 [32, 64, 128], P(('run', 'gx'), 'gy', 'gz'), parts along dimension 0, may hold values from 0 to 1
- well_x: int32 [128], P('run'), parts along dimension 0, may hold values from 0 to 31
- well_y: int32 [128], P('run'), parts along dimension 0, may hold values from 0 to 127
- well_rate: int32 [128], P('run'), parts along dimension 0, may hold values from 1 to 64
- enc_first: bfloat16 [16, 4, 3, 3, 3], replicated, may hold values from -0.625 to 0.625
- enc_second: bfloat16 [16, 16, 3, 3, 3], replicated, may hold values from -0.3125 to 0.3125
- mid_first: bfloat16 [16, 16, 3, 3, 3], replicated, may hold values from -0.3125 to 0.3125
- mid_second: bfloat16 [16, 16, 3, 3, 3], replicated, may hold values from -0.3125 to 0.3125
- dec_weight: bfloat16 [16, 32, 3, 3, 3], replicated, may hold values from -0.21875 to 0.21875
- head_weight: bfloat16 [16], replicated, may hold values from -1.5 to 1.5
Outputs:
- pressure: float32 [64, 128, 256], P(('run', 'gx'), 'gy', 'gz'), parts along dimension 0
- saturation_new: float32 [32, 64, 128], P(('run', 'gx'), 'gy', 'gz'), parts along dimension 0
The draws below stay inside these ranges and needn't reach their ends.
There are 2 independent parts, one for each index of `run`. The reference program is written for one: setup_inputs(seed, part) draws one part's arguments, and reference() takes and returns one part's arrays. A program takes and returns all parts, laid end to end along the dimension named above; an argument that names none is the same for every part. Nothing has to cross between parts.
Inputs may be any that keep to these rules, and one draw needn't show every extreme that they name: facies classes index the tables.
All inputs are finite; a program needn't handle non-finite values.
Results may differ from the reference program's by a relative error of at most 0.0035.
Values may be sent and summed in bfloat16 or wider, within the bound.
A program may use at most 192 MiB of HBM per device.

```python
import jax
import jax.numpy as jnp
from jax import lax

WIDTH = 16
IN_CH = 4
FACIES = 5
WELLS = 64
COARSE_SWEEPS = 8
NX = 32
NY = 128
NZ = 256


def set_ends(array, key, least, largest):
    extent = array.shape
    index_at = [jax.random.randint(jax.random.fold_in(key, axis), (), 0, extent[axis]) for axis in range(len(extent))]
    array = array.at[tuple(index_at)].set(least)
    longest = extent.index(max(extent))
    index_at[longest] = (index_at[longest] + 1) % extent[longest]
    return array.at[tuple(index_at)].set(largest)


def block_levels(key, extent, cuts, least, top_value):
    factor_of, own = 1.0, jax.random.fold_in(key, 6)
    for axis_at, parts in cuts:
        heights = jnp.exp(jax.random.uniform(jax.random.fold_in(own, axis_at), (parts,), jnp.float32, least / len(cuts), top_value / len(cuts)))
        factor_of = factor_of * jnp.repeat(heights, extent[axis_at] // parts).reshape([-1 if axis == axis_at else 1 for axis in range(len(extent))])
    return factor_of


def bell_draw(stream_key, shape, deviation, most, pieces=(), kind=jnp.bfloat16):
    values = jax.random.normal(stream_key, shape, jnp.float32) * deviation
    if len(pieces) > 0:
        values = block_levels(stream_key, shape, pieces, -0.22, 0.18) * values
    return jnp.clip(values, min=-most, max=most).astype(kind)


def setup_inputs(seed: int = 0, part: int = 0) -> dict:
    arg_keys = jax.random.split(jax.random.key(seed), 13)
    part_keys = jax.random.split(jax.random.fold_in(arg_keys[12], part), 13)
    facies = set_ends(jax.random.randint(part_keys[0], (NX, NY, NZ), 0, FACIES), jax.random.fold_in(part_keys[0], 1), 0, FACIES - 1).astype(jnp.int32)
    pressure_old = bell_draw(part_keys[1], (NX, NY, NZ), 1.0, 6.0, ((0, 2), (1, 4), (2, 2)), jnp.float32)
    saturation = jnp.clip(1.0 * jax.random.uniform(part_keys[2], (NX // 2, NY // 2, NZ // 2), jnp.float32) ** block_levels(part_keys[2], (NX // 2, NY // 2, NZ // 2), ((0, 2), (1, 4), (2, 2)), -0.2, 0.2), 0.0, 1.0)
    well_x = set_ends(jax.random.randint(part_keys[3], (WELLS,), 0, NX), jax.random.fold_in(part_keys[3], 1), 0, NX - 1).astype(jnp.int32)
    well_y = set_ends(jax.random.randint(part_keys[4], (WELLS,), 0, NY), jax.random.fold_in(part_keys[4], 1), 0, NY - 1).astype(jnp.int32)
    well_rate = set_ends(jax.random.randint(part_keys[5], (WELLS,), 1, 65), jax.random.fold_in(part_keys[5], 1), 1, 64).astype(jnp.int32)
    enc_first = bell_draw(arg_keys[6], (WIDTH, IN_CH, 3, 3, 3), (27 * IN_CH) ** -0.5, 0.625)
    enc_second = bell_draw(arg_keys[7], (WIDTH, WIDTH, 3, 3, 3), (27 * WIDTH) ** -0.5, 0.3125)
    mid_first = bell_draw(arg_keys[8], (WIDTH, WIDTH, 3, 3, 3), (27 * WIDTH) ** -0.5, 0.3125)
    mid_second = bell_draw(arg_keys[9], (WIDTH, WIDTH, 3, 3, 3), (27 * WIDTH) ** -0.5, 0.3125)
    dec_weight = bell_draw(arg_keys[10], (WIDTH, 2 * WIDTH, 3, 3, 3), (54 * WIDTH) ** -0.5, 0.21875)
    head_weight = bell_draw(arg_keys[11], (WIDTH,), WIDTH ** -0.5, 1.5)
    return {"facies": facies, "pressure_old": pressure_old, "saturation": saturation, "well_x": well_x, "well_y": well_y, "well_rate": well_rate, "enc_first": enc_first, "enc_second": enc_second, "mid_first": mid_first, "mid_second": mid_second, "dec_weight": dec_weight, "head_weight": head_weight}


PERM_TABLE = (0.02, 0.15, 0.8, 2.5, 9.0)
LOG_PERM_TABLE = (-3.912023, -1.89712, -0.223144, 0.916291, 2.197225)
PORE_TABLE = (0.05, 0.12, 0.2, 0.25, 0.3)
storage_factor = 0.0002
vertical_factor = 0.5
relax_weight = 0.6666667
rate_unit = 0.05


def table_lookup(facies, table):
    result = jnp.zeros(facies.shape, jnp.float32)
    for entry_index in range(len(table)):
        result = result + jnp.where(facies == entry_index, jnp.float32(table[entry_index]), jnp.float32(0.0))
    return result


def harmonic(lower, upper):
    return 2.0 * lower * upper / (lower + upper)


def with_diagonal(storage, faces):
    diagonal = storage + faces[0] + faces[1] + faces[2] + faces[3] + faces[4] + faces[5]
    return (storage, faces, diagonal)


def fine_operator(permeability, padded, storage):
    faces = (
        harmonic(padded[:-2, 1:-1, 1:-1], permeability),
        harmonic(permeability, padded[2:, 1:-1, 1:-1]),
        harmonic(padded[1:-1, :-2, 1:-1], permeability),
        harmonic(permeability, padded[1:-1, 2:, 1:-1]),
        vertical_factor * harmonic(padded[1:-1, 1:-1, :-2], permeability),
        vertical_factor * harmonic(permeability, padded[1:-1, 1:-1, 2:]),
    )
    return with_diagonal(storage, faces)


def pair_yz(values):
    size_x, size_y, size_z = values.shape
    return values.reshape(size_x, size_y // 2, 2, size_z // 2, 2).sum(axis=(2, 4))


def pair_xz(values):
    size_x, size_y, size_z = values.shape
    return values.reshape(size_x // 2, 2, size_y, size_z // 2, 2).sum(axis=(1, 4))


def pair_xy(values):
    size_x, size_y, size_z = values.shape
    return values.reshape(size_x // 2, 2, size_y // 2, 2, size_z).sum(axis=(1, 3))


def block_sum(values):
    size_x, size_y, size_z = values.shape
    return values.reshape(size_x // 2, 2, size_y // 2, 2, size_z // 2, 2).sum(axis=(1, 3, 5))


def coarsen_operator(operator):
    storage, faces, diagonal = operator
    new_faces = (
        pair_yz(faces[0][0::2]),
        pair_yz(faces[1][1::2]),
        pair_xz(faces[2][:, 0::2]),
        pair_xz(faces[3][:, 1::2]),
        pair_xy(faces[4][:, :, 0::2]),
        pair_xy(faces[5][:, :, 1::2]),
    )
    return with_diagonal(block_sum(storage), new_faces)


def apply_padded(field, padded, operator):
    storage, faces, diagonal = operator
    beside = faces[0] * padded[:-2, 1:-1, 1:-1] + faces[1] * padded[2:, 1:-1, 1:-1]
    beside = beside + faces[2] * padded[1:-1, :-2, 1:-1] + faces[3] * padded[1:-1, 2:, 1:-1]
    beside = beside + faces[4] * padded[1:-1, 1:-1, :-2] + faces[5] * padded[1:-1, 1:-1, 2:]
    return diagonal * field - beside


def apply_level(field, operator):
    return apply_padded(field, jnp.pad(field, 1), operator)


def relax(field, rhs, operator):
    return field + relax_weight * (rhs - apply_level(field, operator)) / operator[2]


def enlarge(values):
    return jnp.repeat(jnp.repeat(jnp.repeat(values, 2, 0), 2, 1), 2, 2)


def enlarge_channels(values):
    return jnp.repeat(jnp.repeat(jnp.repeat(values, 2, 1), 2, 2), 2, 3)


def well_columns(well_x, well_y, well_rate, start_x, start_y, count_x, count_y):
    along_x = (well_x[:, None] == start_x + jnp.arange(count_x, dtype=jnp.int32)[None, :]).astype(jnp.float32)
    along_y = (well_y[:, None] == start_y + jnp.arange(count_y, dtype=jnp.int32)[None, :]).astype(jnp.float32)
    weighted = along_x * well_rate.astype(jnp.float32)[:, None]
    return jnp.dot(weighted.T, along_y, precision=lax.Precision.HIGHEST)


def pool_mean(values):
    channels, size_x, size_y, size_z = values.shape
    summed = values.astype(jnp.float32).reshape(channels, size_x // 2, 2, size_y // 2, 2, size_z // 2, 2).sum(axis=(2, 4, 6))
    return (summed * 0.125).astype(jnp.bfloat16)


def conv_layer(inputs, weight):
    result = lax.conv_general_dilated(
        inputs[None].astype(jnp.float32), weight.astype(jnp.float32), (1, 1, 1),
        [(1, 1), (1, 1), (1, 1)], dimension_numbers=("NCDHW", "OIDHW", "NCDHW"),
        precision=lax.Precision.HIGHEST)[0]
    return jax.nn.silu(result).astype(jnp.bfloat16)


def reference(facies, pressure_old, saturation, well_x, well_y, well_rate, enc_first, enc_second, mid_first, mid_second, dec_weight, head_weight):
    permeability = table_lookup(facies, PERM_TABLE)
    storage = storage_factor * table_lookup(facies, PORE_TABLE)
    level_zero = fine_operator(permeability, jnp.pad(permeability, 1), storage)
    level_one = coarsen_operator(level_zero)
    level_two = coarsen_operator(level_one)
    level_three = coarsen_operator(level_two)
    column = well_columns(well_x, well_y, well_rate, 0, 0, facies.shape[0], facies.shape[1])
    source = jnp.broadcast_to(rate_unit * column[:, :, None], facies.shape)
    rhs = storage * pressure_old + source

    state_zero = relax(pressure_old, rhs, level_zero)
    rhs_one = block_sum(rhs - apply_level(state_zero, level_zero))
    state_one = relax_weight * rhs_one / level_one[2]
    rhs_two = block_sum(rhs_one - apply_level(state_one, level_one))
    state_two = relax_weight * rhs_two / level_two[2]
    rhs_three = block_sum(rhs_two - apply_level(state_two, level_two))
    state_three = relax_weight * rhs_three / level_three[2]
    for sweep_turn in range(COARSE_SWEEPS - 1):
        state_three = relax(state_three, rhs_three, level_three)
    state_two = relax(state_two + enlarge(state_three), rhs_two, level_two)
    state_one = relax(state_one + enlarge(state_two), rhs_one, level_one)
    pressure = relax(state_zero + enlarge(state_one), rhs, level_zero)

    mean_pressure = block_sum(pressure) * 0.125
    mean_logperm = block_sum(table_lookup(facies, LOG_PERM_TABLE)) * 0.125
    mean_source = block_sum(source) * 0.125
    features = jnp.stack([saturation, mean_pressure, mean_logperm, mean_source]).astype(jnp.bfloat16)
    first = conv_layer(features, enc_first)
    skip = conv_layer(first, enc_second)
    pooled = pool_mean(skip)
    middle = conv_layer(pooled, mid_first)
    deep = conv_layer(middle, mid_second)
    joined = jnp.concatenate([skip, enlarge_channels(deep)], 0)
    decoded = conv_layer(joined, dec_weight)
    channels = decoded.shape[0]
    delta = jnp.dot(head_weight[None, :], decoded.reshape(channels, -1), preferred_element_type=jnp.float32)
    return pressure, saturation + delta.reshape(saturation.shape)
```

```python
import functools

import jax
import jax.numpy as jnp
from jax import lax
from jax.experimental import pallas as pl
from jax.experimental.pallas import tpu as pltpu
from jax.sharding import PartitionSpec as P

COARSE_SWEEPS = 8
PERM_TABLE = (0.02, 0.15, 0.8, 2.5, 9.0)
LOG_PERM_TABLE = (-3.912023, -1.89712, -0.223144, 0.916291, 2.197225)
PORE_TABLE = (0.05, 0.12, 0.2, 0.25, 0.3)
storage_factor = 0.0002
vertical_factor = 0.5
relax_weight = 0.6666667
rate_unit = 0.05
MESH = pl.DeviceIdType.MESH
RIM = 3


def table_lookup(facies, table):
    result = jnp.full(facies.shape, table[0], jnp.float32)
    for entry_index in range(1, len(table)):
        result = jnp.where(facies == entry_index, jnp.float32(table[entry_index]), result)
    return result


def harmonic(lower, upper):
    return 2.0 * lower * upper / (lower + upper)


def pair_x(values):
    size_x, size_y, size_z = values.shape
    split = values.reshape(size_x // 2, 2, size_y, size_z)
    return split[:, 0], split[:, 1]


def turn(values, shift, axis):
    return pltpu.roll(values, shift % values.shape[axis], axis)


def even_cells(shape, step, axis):
    index = lax.broadcasted_iota(jnp.int32, shape, axis)
    return (index & step) == 0


def pair_sum(values, step, axis):
    even = even_cells(values.shape, step, axis)
    return values + jnp.where(even, turn(values, -step, axis), turn(values, step, axis))


def take_even(values, step, axis):
    return jnp.where(even_cells(values.shape, step, axis), values, turn(values, step, axis))


def take_odd(values, step, axis):
    return jnp.where(even_cells(values.shape, step, axis), turn(values, -step, axis), values)


def block_sum(values, step):
    low, high = pair_x(values)
    return pair_sum(pair_sum(low + high, step, 1), step, 2)


def with_diagonal(storage, faces):
    diagonal = storage + faces[0] + faces[1] + faces[2] + faces[3] + faces[4] + faces[5]
    return (storage, faces, diagonal)


def coarsen(operator, step):
    storage, faces, _ = operator
    sides_y = [sum(pair_x(faces[i])) for i in (2, 3)]
    sides_z = [sum(pair_x(faces[i])) for i in (4, 5)]
    new_faces = (
        pair_sum(pair_sum(pair_x(faces[0])[0], step, 1), step, 2),
        pair_sum(pair_sum(pair_x(faces[1])[1], step, 1), step, 2),
        take_even(pair_sum(sides_y[0], step, 2), step, 1),
        take_odd(pair_sum(sides_y[1], step, 2), step, 1),
        take_even(pair_sum(sides_z[0], step, 1), step, 2),
        take_odd(pair_sum(sides_z[1], step, 1), step, 2),
    )
    return with_diagonal(block_sum(storage, step), new_faces)


def enlarge_x(values):
    size_x, size_y, size_z = values.shape
    return jnp.broadcast_to(values[:, None], (size_x, 2, size_y, size_z)).reshape(
        size_x * 2, size_y, size_z
    )


def cycle_kernel(sizes, fac_ref, old_ref, col_ref, out_ref, feat_ref, *scratch):
    levels, (send_sem, recv_sem) = scratch[:-2], scratch[-2:]
    levels = [levels[5 * i : 5 * i + 5] for i in range(4)]
    count_x, count_y = sizes
    at_x, at_y, at_z = (lax.axis_index(axis) for axis in ("gx", "gy", "gz"))
    others = (
        (at_x > 0, {"gx": jnp.maximum(at_x - 1, 0)}),
        (at_x < count_x - 1, {"gx": jnp.minimum(at_x + 1, count_x - 1)}),
        (at_y > 0, {"gy": jnp.maximum(at_y - 1, 0)}),
        (at_y < count_y - 1, {"gy": jnp.minimum(at_y + 1, count_y - 1)}),
    )
    partner = {"gz": 1 - at_z}
    for held, outgoing, beside_x, beside_y, beside_z in levels:
        beside_x[...] = jnp.zeros_like(beside_x)
        beside_y[...] = jnp.zeros_like(beside_y)

    barrier = pltpu.get_barrier_semaphore()
    for there, device in others:

        @pl.when(there)
        def _():
            pl.semaphore_signal(barrier, inc=1, device_id=device, device_id_type=MESH)

    pl.semaphore_signal(barrier, inc=1, device_id=partner, device_id_type=MESH)
    peers = 1 + sum(there.astype(jnp.int32) for there, _ in others)
    pl.semaphore_wait(barrier, peers)

    used = [0, 0, 0, 0]
    turn_of = [0]

    def begin(values, level):
        slot = used[level]
        used[level] += 1
        k = turn_of[0]
        turn_of[0] += 1
        held, outgoing, beside_x, beside_y, beside_z = levels[level]
        size_x, size_y, _ = values.shape
        held[slot] = values
        outgoing[slot, 0] = values[:, :1]
        outgoing[slot, 1] = values[:, size_y - 1 :]
        sources = (
            held.at[slot, pl.ds(0, 1)],
            held.at[slot, pl.ds(size_x - 1, 1)],
            outgoing.at[slot, 0],
            outgoing.at[slot, 1],
        )
        targets = (
            beside_x.at[slot, pl.ds(1, 1)],
            beside_x.at[slot, pl.ds(0, 1)],
            beside_y.at[slot, 1],
            beside_y.at[slot, 0],
        )
        copies = []
        for side, (there, device) in enumerate(others):
            back = side ^ 1
            copy = pltpu.make_async_remote_copy(
                sources[side],
                targets[side],
                send_sem.at[k, side],
                recv_sem.at[k, back],
                device_id=device,
                device_id_type=MESH,
            )
            pl.when(there)(copy.start)
            arrival = pltpu.make_async_remote_copy(
                sources[back],
                targets[back],
                send_sem.at[k, side],
                recv_sem.at[k, side],
                device_id=device,
                device_id_type=MESH,
            )
            copies.append((there, copy, arrival))
        across = pltpu.make_async_remote_copy(
            held.at[slot],
            beside_z.at[slot],
            send_sem.at[k, 4],
            recv_sem.at[k, 4],
            device_id=partner,
            device_id_type=MESH,
        )
        across.start()
        return level, slot, copies, across

    def finish(pending):
        level, slot, copies, across = pending
        for there, copy, arrival in copies:

            @pl.when(there)
            def _():
                copy.wait_send()
                arrival.wait_recv()

        across.wait()
        _, _, beside_x, beside_y, beside_z = levels[level]
        return beside_x[slot], beside_y[slot], beside_z[slot]

    def neighbours(values, beside, step):
        along_x, along_y, along_z = beside
        shape = values.shape
        index_y = lax.broadcasted_iota(jnp.int32, shape, 1)
        index_z = lax.broadcasted_iota(jnp.int32, shape, 2)
        size_y, size_z = shape[1:]
        return (
            jnp.concatenate([along_x[:1], values[:-1]], 0),
            jnp.concatenate([values[1:], along_x[1:]], 0),
            jnp.where(index_y < step, along_y[0], turn(values, step, 1)),
            jnp.where(index_y >= size_y - step, along_y[1], turn(values, -step, 1)),
            turn(jnp.where(index_z >= size_z - step, along_z, values), step, 2),
            turn(jnp.where(index_z < step, along_z, values), -step, 2),
        )

    def apply_with(values, beside, operator, step):
        total = operator[2] * values
        for face, other in zip(operator[1], neighbours(values, beside, step)):
            total = total - face * other
        return total

    def apply_level(values, operator, level):
        return apply_with(values, finish(begin(values, level)), operator, 1 << level)

    def relax(values, rhs, operator, level):
        return values + relax_weight * (rhs - apply_level(values, operator, level)) / operator[2]

    facies = fac_ref[...]
    permeability = table_lookup(facies, PERM_TABLE)
    sent_perm = begin(permeability, 0)
    old = old_ref[...]
    sent_old = begin(old, 0)
    storage = storage_factor * table_lookup(facies, PORE_TABLE)
    source = jnp.broadcast_to(rate_unit * col_ref[...], facies.shape)
    rhs = storage * old + source

    around = list(neighbours(permeability, finish(sent_perm), 1))
    index_z = lax.broadcasted_iota(jnp.int32, facies.shape, 2)
    size_z = facies.shape[2]
    around[4] = jnp.where((index_z == 0) & (at_z == 0), 0.0, around[4])
    around[5] = jnp.where((index_z == size_z - 1) & (at_z == 1), 0.0, around[5])
    faces = [harmonic(permeability, other) for other in around]
    faces[4] = vertical_factor * faces[4]
    faces[5] = vertical_factor * faces[5]
    zero = with_diagonal(storage, faces)
    one = coarsen(zero, 1)
    two = coarsen(one, 2)
    three = coarsen(two, 4)

    product = apply_with(old, finish(sent_old), zero, 1)
    state_zero = old + relax_weight * (rhs - product) / zero[2]
    rhs_one = block_sum(rhs - apply_level(state_zero, zero, 0), 1)
    state_one = relax_weight * rhs_one / one[2]
    rhs_two = block_sum(rhs_one - apply_level(state_one, one, 1), 2)
    state_two = relax_weight * rhs_two / two[2]
    rhs_three = block_sum(rhs_two - apply_level(state_two, two, 2), 4)
    state_three = relax_weight * rhs_three / three[2]
    for _ in range(COARSE_SWEEPS - 1):
        state_three = relax(state_three, rhs_three, three, 3)
    state_two = relax(state_two + enlarge_x(state_three), rhs_two, two, 2)
    state_one = relax(state_one + enlarge_x(state_two), rhs_one, one, 1)
    pressure = relax(state_zero + enlarge_x(state_one), rhs, zero, 0)
    out_ref[...] = pressure

    size_x, size_y, _ = facies.shape
    keep_z = (
        lax.broadcasted_iota(jnp.int32, (size_z, size_z // 2), 0)
        == 2 * lax.broadcasted_iota(jnp.int32, (size_z, size_z // 2), 1)
    ).astype(jnp.bfloat16)
    keep_y = (
        2 * lax.broadcasted_iota(jnp.int32, (size_y // 2, size_y), 0)
        == lax.broadcasted_iota(jnp.int32, (size_y // 2, size_y), 1)
    ).astype(jnp.bfloat16)
    for channel, field in enumerate((pressure, table_lookup(facies, LOG_PERM_TABLE), source)):
        mean = (block_sum(field, 1) * 0.125).astype(jnp.bfloat16)
        for plane in range(size_x // 2):
            rows = jnp.dot(keep_y, mean[plane], preferred_element_type=jnp.float32)
            cells = jnp.dot(
                rows.astype(jnp.bfloat16), keep_z, preferred_element_type=jnp.float32
            )
            feat_ref[channel, plane] = cells


def pressure_cycle(facies, pressure_old, column):
    size_x, size_y, size_z = facies.shape
    counts = (4, 2, 2, COARSE_SWEEPS - 1)
    scratch = []
    for level, count in enumerate(counts):
        planes = size_x >> level
        scratch += [
            pltpu.VMEM((count, planes, size_y, size_z), jnp.float32),
            pltpu.VMEM((count, 2, planes, 1, size_z), jnp.float32),
            pltpu.VMEM((count, 2, size_y, size_z), jnp.float32),
            pltpu.VMEM((count, 2, planes, 1, size_z), jnp.float32),
            pltpu.VMEM((count, planes, size_y, size_z), jnp.float32),
        ]
    turns = sum(counts)
    scratch += [pltpu.SemaphoreType.DMA((turns, 5)), pltpu.SemaphoreType.DMA((turns, 5))]
    return pl.pallas_call(
        functools.partial(cycle_kernel, (lax.axis_size("gx"), lax.axis_size("gy"))),
        out_shape=(
            jax.ShapeDtypeStruct(facies.shape, jnp.float32),
            jax.ShapeDtypeStruct((3, size_x // 2, size_y // 2, size_z // 2), jnp.float32),
        ),
        in_specs=[pl.BlockSpec(memory_space=pltpu.VMEM)] * 3,
        out_specs=[pl.BlockSpec(memory_space=pltpu.VMEM)] * 2,
        scratch_shapes=scratch,
        compiler_params=pltpu.CompilerParams(
            collective_id=0, has_side_effects=True, vmem_limit_bytes=48 * 1024 * 1024
        ),
    )(facies, pressure_old, column)


def well_columns(well_x, well_y, well_rate, start_x, start_y, count_x, count_y):
    along_x = (well_x[:, None] == start_x + jnp.arange(count_x, dtype=jnp.int32)[None, :]).astype(
        jnp.float32
    )
    along_y = (well_y[:, None] == start_y + jnp.arange(count_y, dtype=jnp.int32)[None, :]).astype(
        jnp.float32
    )
    weighted = along_x * well_rate.astype(jnp.float32)[:, None]
    return jnp.dot(weighted.T, along_y, precision=lax.Precision.HIGHEST)


def with_halo(block, sides, width):
    for axis, dim in sides:
        count = lax.axis_size(axis)
        forward = [(i, i + 1) for i in range(count - 1)]
        backward = [(target, source) for source, target in forward]
        low = lax.ppermute(
            lax.slice_in_dim(block, block.shape[dim] - width, None, axis=dim), axis, forward
        )
        high = lax.ppermute(lax.slice_in_dim(block, 0, width, axis=dim), axis, backward)
        block = jnp.concatenate([low, block, high], axis=dim)
    return block


def lanes_of(size_y, size_z):
    return -(-((size_y + 2 * RIM) * (size_z + 2 * RIM)) // 128) * 128


def flat_planes(padded):
    channels, size_x, size_y, size_z = padded.shape
    lanes = lanes_of(size_y - 2 * RIM, size_z - 2 * RIM)
    flat = padded.transpose(1, 0, 2, 3).reshape(size_x, channels, size_y * size_z)
    return jnp.pad(flat, ((0, 0), (0, 0), (0, lanes - size_y * size_z)))


def inside_mask(sizes):
    parts = []
    for size, axis in zip(sizes, ("gx", "gy", "gz")):
        index = jnp.arange(size + 2 * RIM) - RIM + lax.axis_index(axis) * size
        parts.append((index >= 0) & (index < size * lax.axis_size(axis)))
    mask = parts[0][:, None, None] & parts[1][None, :, None] & parts[2][None, None, :]
    return flat_planes(mask[None].astype(jnp.float32))


def flat_index(size_y, size_z):
    lanes = lanes_of(size_y, size_z)
    index = jnp.arange(lanes)
    wide = size_z + 2 * RIM
    real = index < wide * (size_y + 2 * RIM)
    return jnp.where(real, index // wide - RIM, -100), jnp.where(real, index % wide - RIM, -100)


def conv_matrix(weight):
    width, channels = weight.shape[:2]
    groups = -(-channels // 16)
    weight = jnp.pad(weight, ((0, 0), (0, groups * 16 - channels), (0, 0), (0, 0), (0, 0)))
    weight = weight.reshape(width, groups, 16, 3, 3, 3).transpose(4, 5, 0, 1, 3, 2)
    return weight.reshape(9 * width, groups * 48)


def conv_plane(matrix, wide, groups):
    stacked = [g.reshape(g.shape[0] * g.shape[1], g.shape[2]) for g in groups]
    stacked = stacked[0] if len(stacked) == 1 else jnp.concatenate(stacked, 0)
    product = jnp.dot(matrix, stacked, preferred_element_type=jnp.float32)
    lanes = product.shape[1]
    total = None
    for shift in range(9):
        offset = (shift // 3 - 1) * wide + shift % 3 - 1
        part = product[16 * shift : 16 * shift + 16]
        if offset:
            part = pltpu.roll(part, (-offset) % lanes, 1)
        total = part if total is None else total + part
    return total


def silu(values):
    return values / (1.0 + jnp.exp(-values))


def encode_kernel(wide, feat_ref, mask_ref, w1_ref, w2_ref, keep_ref, skip_ref, pool_ref, first):
    planes = feat_ref.shape[0]

    @pl.loop(0, planes - 2)
    def _(x):
        values = silu(conv_plane(w1_ref[...], wide, [feat_ref[pl.ds(x, 3)]]))
        first[x] = (jnp.where(mask_ref[x + 1] > 0, values, 0.0)).astype(jnp.bfloat16)

    @pl.loop(0, planes - 4)
    def _(x):
        values = silu(conv_plane(w2_ref[...], wide, [first[pl.ds(x, 3)]]))
        skip_ref[x] = (jnp.where(mask_ref[x + 2] > 0, values, 0.0)).astype(jnp.bfloat16)

    @pl.loop(0, pool_ref.shape[0])
    def _(x):
        total = skip_ref[2 * x + 1].astype(jnp.float32) + skip_ref[2 * x + 2].astype(jnp.float32)
        lanes = total.shape[1]
        total = total + pltpu.roll(total, lanes - 1, 1)
        total = total + pltpu.roll(total, lanes - wide, 1)
        mean = (total * 0.125).astype(jnp.bfloat16)
        pool_ref[x] = jnp.dot(mean, keep_ref[...], preferred_element_type=jnp.float32).astype(
            jnp.bfloat16
        )


def decode_kernel(
    wide, wide_pool, skip_ref, pool_ref, mask_ref, w1_ref, w2_ref, w3_ref, head_ref, up_ref,
    delta_ref, middle, deep, raised,
):
    planes = pool_ref.shape[0]

    @pl.loop(0, planes - 2)
    def _(x):
        values = silu(conv_plane(w1_ref[...], wide_pool, [pool_ref[pl.ds(x, 3)]]))
        middle[x] = (jnp.where(mask_ref[x + 1] > 0, values, 0.0)).astype(jnp.bfloat16)

    @pl.loop(0, planes - 4)
    def _(x):
        values = silu(conv_plane(w2_ref[...], wide_pool, [middle[pl.ds(x, 3)]]))
        values = jnp.where(mask_ref[x + 2] > 0, values, 0.0).astype(jnp.bfloat16)
        deep[x] = jnp.dot(values, up_ref[...], preferred_element_type=jnp.float32).astype(
            jnp.bfloat16
        )

    for x in range(raised.shape[0]):
        raised[x] = deep[(x + 1) // 2]

    @pl.loop(0, delta_ref.shape[0])
    def _(x):
        values = silu(
            conv_plane(w3_ref[...], wide, [skip_ref[pl.ds(x, 3)], raised[pl.ds(x, 3)]])
        )
        values = values.astype(jnp.bfloat16).astype(jnp.float32)
        delta_ref[x] = jnp.sum(values * head_ref[...], axis=0, keepdims=True)


def on_device(
    facies, pressure_old, saturation, well_x, well_y, well_rate,
    enc_first, enc_second, mid_first, mid_second, dec_weight, head_weight,
):
    size_x, size_y, size_z = facies.shape
    column = well_columns(
        well_x, well_y, well_rate,
        lax.axis_index("gx") * size_x, lax.axis_index("gy") * size_y, size_x, size_y,
    )
    pressure, means = pressure_cycle(facies, pressure_old, column[:, :, None])
    blocks = saturation.shape
    pools = tuple(size // 2 for size in blocks)
    sides = (("gy", 2), ("gx", 1), ("gz", 3))
    features = jnp.concatenate([saturation[None], means], 0).astype(jnp.bfloat16)
    features = with_halo(features, sides, RIM)
    features = jnp.pad(features, ((0, 12), (0, 0), (0, 0), (0, 0)))
    planes = flat_planes(features)
    lanes, lanes_pool = lanes_of(*blocks[1:]), lanes_of(*pools[1:])
    wide, wide_pool = blocks[2] + 2 * RIM, pools[2] + 2 * RIM

    row, depth = flat_index(*blocks[1:])
    row_pool, depth_pool = flat_index(*pools[1:])
    own = jnp.arange(pools[1] * pools[2])
    keep = (
        (row[:, None] == 2 * (own // pools[2])[None]) & (depth[:, None] == 2 * (own % pools[2])[None])
    ).astype(jnp.bfloat16)
    raise_matrix = (
        (row_pool[:, None] == jnp.floor_divide(row, 2)[None])
        & (depth_pool[:, None] == jnp.floor_divide(depth, 2)[None])
        & (row_pool > -100)[:, None]
    ).astype(jnp.bfloat16)

    whole = pl.BlockSpec(memory_space=pltpu.VMEM)
    limit = pltpu.CompilerParams(vmem_limit_bytes=48 * 1024 * 1024)
    skip, pooled = pl.pallas_call(
        functools.partial(encode_kernel, wide),
        out_shape=(
            jax.ShapeDtypeStruct((blocks[0] + 2, 16, lanes), jnp.bfloat16),
            jax.ShapeDtypeStruct((pools[0], 16, pools[1] * pools[2]), jnp.bfloat16),
        ),
        in_specs=[whole] * 5,
        out_specs=[whole] * 2,
        scratch_shapes=[pltpu.VMEM((blocks[0] + 4, 16, lanes), jnp.bfloat16)],
        compiler_params=limit,
    )(planes, inside_mask(blocks), conv_matrix(enc_first), conv_matrix(enc_second), keep)
    pooled = pooled.transpose(1, 0, 2).reshape(16, *pools)
    pooled = flat_planes(with_halo(pooled, sides, RIM))
    delta = pl.pallas_call(
        functools.partial(decode_kernel, wide, wide_pool),
        out_shape=jax.ShapeDtypeStruct((blocks[0], 1, lanes), jnp.float32),
        in_specs=[whole] * 8,
        out_specs=whole,
        scratch_shapes=[
            pltpu.VMEM((pools[0] + 4, 16, lanes_pool), jnp.bfloat16),
            pltpu.VMEM((pools[0] + 2, 16, lanes), jnp.bfloat16),
            pltpu.VMEM((blocks[0] + 2, 16, lanes), jnp.bfloat16),
        ],
        compiler_params=limit,
    )(
        skip, pooled, inside_mask(pools), conv_matrix(mid_first), conv_matrix(mid_second),
        conv_matrix(dec_weight), head_weight.astype(jnp.float32)[:, None], raise_matrix,
    )
    delta = delta[:, 0, : wide * (blocks[1] + 2 * RIM)]
    delta = delta.reshape(blocks[0], blocks[1] + 2 * RIM, wide)
    delta = delta[:, RIM : RIM + blocks[1], RIM : RIM + blocks[2]]
    return (pressure, saturation + delta)


def solution(mesh):
    return jax.shard_map(
        on_device,
        mesh=mesh,
        in_specs=(P(("run", "gx"), "gy", "gz"),) * 3 + (P("run"),) * 3 + (P(),) * 6,
        out_specs=(P(("run", "gx"), "gy", "gz"), P(("run", "gx"), "gy", "gz")),
        check_vma=False,
    )
```

```python
import functools

import jax
import jax.numpy as jnp
import ml_dtypes
import numpy as np
from jax import lax
from jax.experimental import pallas as pl
from jax.experimental.pallas import tpu as pltpu
from jax.sharding import PartitionSpec as P

COARSE_SWEEPS = 8
PERM_TABLE = (0.02, 0.15, 0.8, 2.5, 9.0)
LOG_PERM_TABLE = (-3.912023, -1.89712, -0.223144, 0.916291, 2.197225)
PORE_TABLE = (0.05, 0.12, 0.2, 0.25, 0.3)
storage_factor = 0.0002
vertical_factor = 0.5
relax_weight = 0.6666667
rate_unit = 0.05
MESH = pl.DeviceIdType.MESH
RIM = 3


def table_lookup(facies, table):
    result = jnp.full(facies.shape, table[0], jnp.float32)
    for entry_index in range(1, len(table)):
        result = jnp.where(facies == entry_index, jnp.float32(table[entry_index]), result)
    return result


def harmonic(lower, upper):
    return 2.0 * lower * upper / (lower + upper)


def pair_x(values):
    size_x, size_y, size_z = values.shape
    split = values.reshape(size_x // 2, 2, size_y, size_z)
    return split[:, 0], split[:, 1]


def turn(values, shift, axis):
    return pltpu.roll(values, shift % values.shape[axis], axis)


def even_cells(shape, step, axis):
    index = lax.broadcasted_iota(jnp.int32, shape, axis)
    return (index & step) == 0


def pair_sum(values, step, axis):
    even = even_cells(values.shape, step, axis)
    return values + jnp.where(even, turn(values, -step, axis), turn(values, step, axis))


def take_even(values, step, axis):
    return jnp.where(even_cells(values.shape, step, axis), values, turn(values, step, axis))


def take_odd(values, step, axis):
    return jnp.where(even_cells(values.shape, step, axis), turn(values, -step, axis), values)


def block_sum(values, step):
    low, high = pair_x(values)
    return pair_sum(pair_sum(low + high, step, 1), step, 2)


def with_diagonal(storage, faces):
    diagonal = storage + faces[0] + faces[1] + faces[2] + faces[3] + faces[4] + faces[5]
    return (storage, faces, diagonal)


def coarsen(operator, step):
    storage, faces, _ = operator
    sides_y = [sum(pair_x(faces[i])) for i in (2, 3)]
    sides_z = [sum(pair_x(faces[i])) for i in (4, 5)]
    new_faces = (
        pair_sum(pair_sum(pair_x(faces[0])[0], step, 1), step, 2),
        pair_sum(pair_sum(pair_x(faces[1])[1], step, 1), step, 2),
        take_even(pair_sum(sides_y[0], step, 2), step, 1),
        take_odd(pair_sum(sides_y[1], step, 2), step, 1),
        take_even(pair_sum(sides_z[0], step, 1), step, 2),
        take_odd(pair_sum(sides_z[1], step, 1), step, 2),
    )
    return with_diagonal(block_sum(storage, step), new_faces)


def enlarge_x(values):
    size_x, size_y, size_z = values.shape
    return jnp.broadcast_to(values[:, None], (size_x, 2, size_y, size_z)).reshape(
        size_x * 2, size_y, size_z
    )


def cycle_kernel(sizes, fac_ref, old_ref, col_ref, out_ref, feat_ref, *scratch):
    levels, (send_sem, recv_sem) = scratch[:-2], scratch[-2:]
    levels = [levels[5 * i : 5 * i + 5] for i in range(4)]
    count_x, count_y = sizes
    at_x, at_y, at_z = (lax.axis_index(axis) for axis in ("gx", "gy", "gz"))
    others = (
        (at_x > 0, {"gx": jnp.maximum(at_x - 1, 0)}),
        (at_x < count_x - 1, {"gx": jnp.minimum(at_x + 1, count_x - 1)}),
        (at_y > 0, {"gy": jnp.maximum(at_y - 1, 0)}),
        (at_y < count_y - 1, {"gy": jnp.minimum(at_y + 1, count_y - 1)}),
    )
    partner = {"gz": 1 - at_z}
    for held, outgoing, beside_x, beside_y, beside_z in levels:
        beside_x[...] = jnp.zeros_like(beside_x)
        beside_y[...] = jnp.zeros_like(beside_y)

    barrier = pltpu.get_barrier_semaphore()
    for there, device in others:

        @pl.when(there)
        def _():
            pl.semaphore_signal(barrier, inc=1, device_id=device, device_id_type=MESH)

    pl.semaphore_signal(barrier, inc=1, device_id=partner, device_id_type=MESH)
    peers = 1 + sum(there.astype(jnp.int32) for there, _ in others)
    pl.semaphore_wait(barrier, peers)

    used = [0, 0, 0, 0]
    turn_of = [0]

    def begin(values, level):
        slot = used[level]
        used[level] += 1
        k = turn_of[0]
        turn_of[0] += 1
        held, outgoing, beside_x, beside_y, beside_z = levels[level]
        size_x, size_y, _ = values.shape
        held[slot] = values
        outgoing[slot, 0] = values[:, :1]
        outgoing[slot, 1] = values[:, size_y - 1 :]
        sources = (
            held.at[slot, pl.ds(0, 1)],
            held.at[slot, pl.ds(size_x - 1, 1)],
            outgoing.at[slot, 0],
            outgoing.at[slot, 1],
        )
        targets = (
            beside_x.at[slot, pl.ds(1, 1)],
            beside_x.at[slot, pl.ds(0, 1)],
            beside_y.at[slot, 1],
            beside_y.at[slot, 0],
        )
        copies = []
        for side, (there, device) in enumerate(others):
            back = side ^ 1
            copy = pltpu.make_async_remote_copy(
                sources[side],
                targets[side],
                send_sem.at[k, side],
                recv_sem.at[k, back],
                device_id=device,
                device_id_type=MESH,
            )
            pl.when(there)(copy.start)
            arrival = pltpu.make_async_remote_copy(
                sources[back],
                targets[back],
                send_sem.at[k, side],
                recv_sem.at[k, side],
                device_id=device,
                device_id_type=MESH,
            )
            copies.append((there, copy, arrival))
        across = pltpu.make_async_remote_copy(
            held.at[slot],
            beside_z.at[slot],
            send_sem.at[k, 4],
            recv_sem.at[k, 4],
            device_id=partner,
            device_id_type=MESH,
        )
        across.start()
        return level, slot, copies, across

    def finish(pending):
        level, slot, copies, across = pending
        for there, copy, arrival in copies:

            @pl.when(there)
            def _():
                copy.wait_send()
                arrival.wait_recv()

        across.wait()
        _, _, beside_x, beside_y, beside_z = levels[level]
        return beside_x[slot], beside_y[slot], beside_z[slot]

    def neighbours(values, beside, step):
        along_x, along_y, along_z = beside
        shape = values.shape
        index_y = lax.broadcasted_iota(jnp.int32, shape, 1)
        index_z = lax.broadcasted_iota(jnp.int32, shape, 2)
        size_y, size_z = shape[1:]
        return (
            jnp.concatenate([along_x[:1], values[:-1]], 0),
            jnp.concatenate([values[1:], along_x[1:]], 0),
            jnp.where(index_y < step, along_y[0], turn(values, step, 1)),
            jnp.where(index_y >= size_y - step, along_y[1], turn(values, -step, 1)),
            turn(jnp.where(index_z >= size_z - step, along_z, values), step, 2),
            turn(jnp.where(index_z < step, along_z, values), -step, 2),
        )

    def apply_with(values, beside, operator, step):
        total = operator[2] * values
        for face, other in zip(operator[1], neighbours(values, beside, step)):
            total = total - face * other
        return total

    def apply_level(values, operator, level):
        return apply_with(values, finish(begin(values, level)), operator, 1 << level)

    def relax(values, rhs, operator, level):
        return values + relax_weight * (rhs - apply_level(values, operator, level)) / operator[2]

    facies = fac_ref[...]
    permeability = table_lookup(facies, PERM_TABLE)
    sent_perm = begin(permeability, 0)
    old = old_ref[...]
    sent_old = begin(old, 0)
    storage = storage_factor * table_lookup(facies, PORE_TABLE)
    source = jnp.broadcast_to(rate_unit * col_ref[...], facies.shape)
    rhs = storage * old + source

    around = list(neighbours(permeability, finish(sent_perm), 1))
    index_z = lax.broadcasted_iota(jnp.int32, facies.shape, 2)
    size_z = facies.shape[2]
    around[4] = jnp.where((index_z == 0) & (at_z == 0), 0.0, around[4])
    around[5] = jnp.where((index_z == size_z - 1) & (at_z == 1), 0.0, around[5])
    faces = [harmonic(permeability, other) for other in around]
    faces[4] = vertical_factor * faces[4]
    faces[5] = vertical_factor * faces[5]
    zero = with_diagonal(storage, faces)
    one = coarsen(zero, 1)
    two = coarsen(one, 2)
    three = coarsen(two, 4)

    product = apply_with(old, finish(sent_old), zero, 1)
    state_zero = old + relax_weight * (rhs - product) / zero[2]
    rhs_one = block_sum(rhs - apply_level(state_zero, zero, 0), 1)
    state_one = relax_weight * rhs_one / one[2]
    rhs_two = block_sum(rhs_one - apply_level(state_one, one, 1), 2)
    state_two = relax_weight * rhs_two / two[2]
    rhs_three = block_sum(rhs_two - apply_level(state_two, two, 2), 4)
    state_three = relax_weight * rhs_three / three[2]
    for _ in range(COARSE_SWEEPS - 1):
        state_three = relax(state_three, rhs_three, three, 3)
    state_two = relax(state_two + enlarge_x(state_three), rhs_two, two, 2)
    state_one = relax(state_one + enlarge_x(state_two), rhs_one, one, 1)
    pressure = relax(state_zero + enlarge_x(state_one), rhs, zero, 0)
    out_ref[...] = pressure

    size_x, size_y, _ = facies.shape
    keep_z = (
        lax.broadcasted_iota(jnp.int32, (size_z, size_z // 2), 0)
        == 2 * lax.broadcasted_iota(jnp.int32, (size_z, size_z // 2), 1)
    ).astype(jnp.bfloat16)
    keep_y = (
        2 * lax.broadcasted_iota(jnp.int32, (size_y // 2, size_y), 0)
        == lax.broadcasted_iota(jnp.int32, (size_y // 2, size_y), 1)
    ).astype(jnp.bfloat16)
    for channel, field in enumerate((pressure, table_lookup(facies, LOG_PERM_TABLE), source)):
        mean = (block_sum(field, 1) * 0.125).astype(jnp.bfloat16)
        for plane in range(size_x // 2):
            rows = jnp.dot(keep_y, mean[plane], preferred_element_type=jnp.float32)
            cells = jnp.dot(
                rows.astype(jnp.bfloat16), keep_z, preferred_element_type=jnp.float32
            )
            feat_ref[channel, plane] = cells


def pressure_cycle(facies, pressure_old, column):
    size_x, size_y, size_z = facies.shape
    counts = (4, 2, 2, COARSE_SWEEPS - 1)
    scratch = []
    for level, count in enumerate(counts):
        planes = size_x >> level
        scratch += [
            pltpu.VMEM((count, planes, size_y, size_z), jnp.float32),
            pltpu.VMEM((count, 2, planes, 1, size_z), jnp.float32),
            pltpu.VMEM((count, 2, size_y, size_z), jnp.float32),
            pltpu.VMEM((count, 2, planes, 1, size_z), jnp.float32),
            pltpu.VMEM((count, planes, size_y, size_z), jnp.float32),
        ]
    turns = sum(counts)
    scratch += [pltpu.SemaphoreType.DMA((turns, 5)), pltpu.SemaphoreType.DMA((turns, 5))]
    return pl.pallas_call(
        functools.partial(cycle_kernel, (lax.axis_size("gx"), lax.axis_size("gy"))),
        out_shape=(
            jax.ShapeDtypeStruct(facies.shape, jnp.float32),
            jax.ShapeDtypeStruct((3, size_x // 2, size_y // 2, size_z // 2), jnp.float32),
        ),
        in_specs=[pl.BlockSpec(memory_space=pltpu.VMEM)] * 3,
        out_specs=[pl.BlockSpec(memory_space=pltpu.VMEM)] * 2,
        scratch_shapes=scratch,
        compiler_params=pltpu.CompilerParams(
            collective_id=0, has_side_effects=True, vmem_limit_bytes=48 * 1024 * 1024
        ),
    )(facies, pressure_old, column)


def well_columns(well_x, well_y, well_rate, start_x, start_y, count_x, count_y):
    along_x = (well_x[:, None] == start_x + jnp.arange(count_x, dtype=jnp.int32)[None, :]).astype(
        jnp.float32
    )
    along_y = (well_y[:, None] == start_y + jnp.arange(count_y, dtype=jnp.int32)[None, :]).astype(
        jnp.float32
    )
    weighted = along_x * well_rate.astype(jnp.float32)[:, None]
    return jnp.dot(weighted.T, along_y, precision=lax.Precision.HIGHEST)


def lanes_of(size_y, size_z):
    return -(-((size_y + 2 * RIM) * (size_z + 2 * RIM)) // 128) * 128


def flat_index(size_y, size_z):
    index = np.arange(lanes_of(size_y, size_z))
    wide = size_z + 2 * RIM
    real = index < wide * (size_y + 2 * RIM)
    row = np.where(real, index // wide - RIM, -100)
    depth = np.where(real, index % wide - RIM, -100)
    return row.astype(np.int32), depth.astype(np.int32)


def own_planes(values):
    channels, size_x, size_y, size_z = values.shape
    lanes = lanes_of(size_y, size_z)
    wide = size_z + 2 * RIM
    padded = jnp.pad(values, ((0, 16 - channels), (0, 0), (0, 0), (0, 2 * RIM)))
    flat = padded.transpose(1, 0, 2, 3).reshape(size_x, 16, size_y * wide)
    start = RIM * wide + RIM
    return jnp.pad(flat, ((0, 0), (0, 0), (start, lanes - start - size_y * wide)))


def conv_matrices(*weights):
    groups = []
    for weight in weights:
        channels = weight.shape[1]
        if channels < 16:
            weight = jnp.pad(weight, ((0, 0), (0, 16 - channels), (0, 0), (0, 0), (0, 0)))
        groups += [weight[:, at : at + 16] for at in range(0, weight.shape[1], 16)]
    stacked = jnp.stack(groups).reshape(len(groups), 16, 16, 3, 9)
    return stacked.transpose(0, 4, 1, 3, 2).reshape(len(groups), 144, 48)


def silu(values):
    return values / (1.0 + jnp.exp(-values))


def network_kernel(
    sizes, blocks, feat_ref, weight_ref, index_ref, pool_index_ref, keep_ref, up_ref, head_ref,
    delta_ref, fields, first, skip, pooled, middle, deep, raised,
    own, own_pool, far, far_pool, rows_in, rows_in_pool, rows_out, rows_out_pool,
    send_sem, recv_sem,
):
    count_x, count_y = sizes
    at_x, at_y, at_z = (lax.axis_index(axis) for axis in ("gx", "gy", "gz"))
    lower = {"gx": jnp.maximum(at_x - 1, 0)}, {"gy": jnp.maximum(at_y - 1, 0)}
    upper = (
        {"gx": jnp.minimum(at_x + 1, count_x - 1)},
        {"gy": jnp.minimum(at_y + 1, count_y - 1)},
    )
    has = ((at_x > 0, at_x < count_x - 1), (at_y > 0, at_y < count_y - 1))
    partner = {"gz": 1 - at_z}
    for ref in (fields, pooled, rows_in, rows_in_pool):
        ref[...] = jnp.zeros_like(ref)

    barrier = pltpu.get_barrier_semaphore()
    for axis in range(2):
        for there, device in ((has[axis][0], lower[axis]), (has[axis][1], upper[axis])):

            @pl.when(there)
            def _():
                pl.semaphore_signal(barrier, inc=1, device_id=device, device_id_type=MESH)

    pl.semaphore_signal(barrier, inc=1, device_id=partner, device_id_type=MESH)
    peers = 1 + sum(there.astype(jnp.int32) for pair in has for there in pair)
    pl.semaphore_wait(barrier, peers)

    def swap(k, axis, to_low, from_low, to_high, from_high):
        low = pltpu.make_async_remote_copy(
            to_low, from_high, send_sem.at[k, 0], recv_sem.at[k, 1],
            device_id=lower[axis], device_id_type=MESH,
        )
        high = pltpu.make_async_remote_copy(
            to_high, from_low, send_sem.at[k, 1], recv_sem.at[k, 0],
            device_id=upper[axis], device_id_type=MESH,
        )
        pl.when(has[axis][0])(low.start)
        pl.when(has[axis][1])(high.start)

        @pl.when(has[axis][0])
        def _():
            low.wait_send()
            high.wait_recv()

        @pl.when(has[axis][1])
        def _():
            high.wait_send()
            low.wait_recv()

    def fill_rims(k, mine, beyond, sent, landed, whole, row, depth, size_y, size_z):
        lanes = mine.shape[2]
        wide = size_z + 2 * RIM
        across = pltpu.make_async_remote_copy(
            mine, beyond, send_sem.at[k, 0], recv_sem.at[k, 0],
            device_id=partner, device_id_type=MESH,
        )
        across.start()
        across.wait()
        planes = mine.shape[0]
        here = (row >= 0) & (row < size_y)
        from_high = here & (depth >= size_z) & (at_z == 0)
        from_low = here & (depth < 0) & (at_z == 1)
        low_at, low_len = low_lanes(size_y, size_z)
        high_at, high_len = high_lanes(size_y, size_z)
        for x in range(planes):
            other = beyond[x].astype(jnp.float32)
            values = mine[x].astype(jnp.float32)
            values = jnp.where(from_high, pltpu.roll(other, size_z, 1), values)
            values = jnp.where(from_low, pltpu.roll(other, lanes - size_z, 1), values)
            values = values.astype(jnp.bfloat16)
            whole[x + RIM] = values
            sent[0, x, :, :low_len] = values[:, low_at : low_at + low_len]
            sent[1, x, :, :high_len] = values[:, high_at : high_at + high_len]
        swap(k + 1, 1, sent.at[0], landed.at[0], sent.at[1], landed.at[1])
        for x in range(planes):
            values = whole[x + RIM].astype(jnp.float32)
            above = jnp.concatenate(
                [landed[0, x].astype(jnp.float32), jnp.zeros((16, lanes - landed.shape[3]), jnp.float32)], 1
            )
            below = jnp.concatenate(
                [landed[1, x].astype(jnp.float32), jnp.zeros((16, lanes - landed.shape[3]), jnp.float32)], 1
            )
            above = pltpu.roll(above, (high_at - size_y * wide) % lanes, 1)
            below = pltpu.roll(below, (low_at + size_y * wide) % lanes, 1)
            values = jnp.where((row < 0) & (row >= -RIM), above, values)
            values = jnp.where(row >= size_y, below, values)
            whole[x + RIM] = values.astype(jnp.bfloat16)
        swap(
            k + 2, 0,
            whole.at[pl.ds(RIM, RIM)], whole.at[pl.ds(0, RIM)],
            whole.at[pl.ds(planes, RIM)], whole.at[pl.ds(planes + RIM, RIM)],
        )

    def on_grid(row, depth, size_y, size_z):
        row, depth = row + at_y * size_y, depth + at_z * size_z
        return (row >= 0) & (row < size_y * count_y) & (depth >= 0) & (depth < 2 * size_z)

    def conv(wide, pieces):
        product = None
        for group, planes in pieces:
            stacked = planes.reshape(48, planes.shape[2])
            term = jnp.dot(weight_ref[group], stacked, preferred_element_type=jnp.float32)
            product = term if product is None else product + term
        lanes = product.shape[1]
        total = None
        for shift in range(9):
            offset = (shift // 3 - 1) * wide + shift % 3 - 1
            part = product[16 * shift : 16 * shift + 16]
            if offset:
                part = pltpu.roll(part, (-offset) % lanes, 1)
            total = part if total is None else total + part
        return silu(total)

    size_x, size_y, size_z = blocks
    pool_x, pool_y, pool_z = (size // 2 for size in blocks)
    wide, wide_pool = size_z + 2 * RIM, pool_z + 2 * RIM
    row, depth = index_ref[0:1], index_ref[1:2]
    row_pool, depth_pool = pool_index_ref[0:1], pool_index_ref[1:2]
    grid = on_grid(row, depth, size_y, size_z)
    grid_pool = on_grid(row_pool, depth_pool, pool_y, pool_z)

    def masked(values, mask, plane, size):
        plane = plane + at_x * size
        inside = jnp.where((plane >= 0) & (plane < size * count_x), 1.0, 0.0)
        return (jnp.where(mask, values, 0.0) * inside).astype(jnp.bfloat16)

    own[...] = feat_ref[...]
    fill_rims(0, own, far, rows_out, rows_in, fields, row, depth, size_y, size_z)

    @pl.loop(0, size_x + 4)
    def _(x):
        first[x] = masked(conv(wide, [(0, fields[pl.ds(x, 3)])]), grid, x - 2, size_x)

    @pl.loop(0, size_x + 2)
    def _(x):
        skip[x] = masked(conv(wide, [(1, first[pl.ds(x, 3)])]), grid, x - 1, size_x)

    @pl.loop(0, pool_x)
    def _(x):
        total = skip[2 * x + 1].astype(jnp.float32) + skip[2 * x + 2].astype(jnp.float32)
        lanes = total.shape[1]
        total = total + pltpu.roll(total, lanes - 1, 1)
        total = total + pltpu.roll(total, lanes - wide, 1)
        mean = (total * 0.125).astype(jnp.bfloat16)
        own_pool[x] = jnp.dot(mean, keep_ref[...], preferred_element_type=jnp.float32).astype(
            jnp.bfloat16
        )

    fill_rims(
        3, own_pool, far_pool, rows_out_pool, rows_in_pool, pooled, row_pool, depth_pool,
        pool_y, pool_z,
    )

    @pl.loop(0, pool_x + 4)
    def _(x):
        middle[x] = masked(conv(wide_pool, [(2, pooled[pl.ds(x, 3)])]), grid_pool, x - 2, pool_x)

    @pl.loop(0, pool_x + 2)
    def _(x):
        values = masked(conv(wide_pool, [(3, middle[pl.ds(x, 3)])]), grid_pool, x - 1, pool_x)
        deep[x] = jnp.dot(values, up_ref[...], preferred_element_type=jnp.float32).astype(
            jnp.bfloat16
        )

    for x in range(size_x + 2):
        raised[x] = deep[(x + 1) // 2]

    @pl.loop(0, size_x)
    def _(x):
        values = conv(wide, [(4, skip[pl.ds(x, 3)]), (5, raised[pl.ds(x, 3)])])
        values = values.astype(jnp.bfloat16).astype(jnp.float32)
        delta_ref[x] = jnp.sum(values * head_ref[...], axis=0, keepdims=True)


def low_lanes(size_y, size_z):
    wide = size_z + 2 * RIM
    start = RIM * wide // 128 * 128
    return start, -(-(2 * RIM * wide) // 128) * 128 - start


def high_lanes(size_y, size_z):
    wide = size_z + 2 * RIM
    start = size_y * wide // 128 * 128
    return start, -(-((size_y + RIM) * wide) // 128) * 128 - start


def network(features, weights, head, blocks):
    pools = tuple(size // 2 for size in blocks)
    lanes, lanes_pool = lanes_of(*blocks[1:]), lanes_of(*pools[1:])
    edge, edge_pool = (
        max(low_lanes(*s[1:])[1], high_lanes(*s[1:])[1]) for s in (blocks, pools)
    )
    row, depth = flat_index(*blocks[1:])
    row_pool, depth_pool = flat_index(*pools[1:])
    owned = (row_pool >= 0) & (row_pool < pools[1]) & (depth_pool >= 0) & (depth_pool < pools[2])
    keep = (row[:, None] == 2 * row_pool[None]) & (depth[:, None] == 2 * depth_pool[None])
    keep = (keep & owned[None]).astype(ml_dtypes.bfloat16)
    up = (row_pool[:, None] == (row // 2)[None]) & (depth_pool[:, None] == (depth // 2)[None])
    up = (up & (row_pool > -100)[:, None]).astype(ml_dtypes.bfloat16)
    whole = pl.BlockSpec(memory_space=pltpu.VMEM)
    x, px, half = blocks[0], pools[0], jnp.bfloat16
    return pl.pallas_call(
        functools.partial(network_kernel, (lax.axis_size("gx"), lax.axis_size("gy")), blocks),
        out_shape=jax.ShapeDtypeStruct((x, 1, lanes), jnp.float32),
        in_specs=[whole] * 7,
        out_specs=whole,
        scratch_shapes=[
            pltpu.VMEM((x + 2 * RIM, 16, lanes), half),
            pltpu.VMEM((x + 4, 16, lanes), half),
            pltpu.VMEM((x + 2, 16, lanes), half),
            pltpu.VMEM((px + 2 * RIM, 16, lanes_pool), half),
            pltpu.VMEM((px + 4, 16, lanes_pool), half),
            pltpu.VMEM((px + 2, 16, lanes), half),
            pltpu.VMEM((x + 2, 16, lanes), half),
            pltpu.VMEM((x, 16, lanes), half),
            pltpu.VMEM((px, 16, lanes_pool), half),
            pltpu.VMEM((x, 16, lanes), half),
            pltpu.VMEM((px, 16, lanes_pool), half),
            pltpu.VMEM((2, x, 16, edge), half),
            pltpu.VMEM((2, px, 16, edge_pool), half),
            pltpu.VMEM((2, x, 16, edge), half),
            pltpu.VMEM((2, px, 16, edge_pool), half),
            pltpu.SemaphoreType.DMA((6, 2)),
            pltpu.SemaphoreType.DMA((6, 2)),
        ],
        compiler_params=pltpu.CompilerParams(
            collective_id=1, has_side_effects=True, vmem_limit_bytes=48 * 1024 * 1024
        ),
    )(
        features, weights, jnp.asarray(np.stack([row, depth])),
        jnp.asarray(np.stack([row_pool, depth_pool])), jnp.asarray(keep), jnp.asarray(up), head,
    )


def on_device(
    facies, pressure_old, saturation, well_x, well_y, well_rate,
    enc_first, enc_second, mid_first, mid_second, dec_weight, head_weight,
):
    size_x, size_y, size_z = facies.shape
    column = well_columns(
        well_x, well_y, well_rate,
        lax.axis_index("gx") * size_x, lax.axis_index("gy") * size_y, size_x, size_y,
    )
    pressure, means = pressure_cycle(facies, pressure_old, column[:, :, None])
    blocks = saturation.shape
    wide = blocks[2] + 2 * RIM
    features = jnp.concatenate([saturation[None], means], 0).astype(jnp.bfloat16)
    weights = conv_matrices(enc_first, enc_second, mid_first, mid_second, dec_weight)
    delta = network(
        own_planes(features), weights, head_weight.astype(jnp.float32)[:, None], blocks
    )
    delta = delta[:, 0, RIM * wide + RIM : RIM * wide + RIM + blocks[1] * wide]
    delta = delta.reshape(blocks[0], blocks[1], wide)[:, :, : blocks[2]]
    return (pressure, saturation + delta)


def solution(mesh):
    return jax.shard_map(
        on_device,
        mesh=mesh,
        in_specs=(P(("run", "gx"), "gy", "gz"),) * 3 + (P("run"),) * 3 + (P(),) * 6,
        out_specs=(P(("run", "gx"), "gy", "gz"), P(("run", "gx"), "gy", "gz")),
        check_vma=False,
    )
```

```python
import functools

import jax
import jax.numpy as jnp
import ml_dtypes
import numpy as np
from jax import lax
from jax.experimental import pallas as pl
from jax.experimental.pallas import tpu as pltpu
from jax.sharding import PartitionSpec as P

COARSE_SWEEPS = 8
PERM_TABLE = (0.02, 0.15, 0.8, 2.5, 9.0)
LOG_PERM_TABLE = (-3.912023, -1.89712, -0.223144, 0.916291, 2.197225)
PORE_TABLE = (0.05, 0.12, 0.2, 0.25, 0.3)
storage_factor = 0.0002
vertical_factor = 0.5
relax_weight = 0.6666667
rate_unit = 0.05
MESH = pl.DeviceIdType.MESH
RIM = 3


def table_lookup(facies, table):
    result = jnp.full(facies.shape, table[0], jnp.float32)
    for entry_index in range(1, len(table)):
        result = jnp.where(facies == entry_index, jnp.float32(table[entry_index]), result)
    return result


def harmonic(lower, upper):
    return 2.0 * lower * upper / (lower + upper)


def pair_x(values):
    size_x, size_y, size_z = values.shape
    split = values.reshape(size_x // 2, 2, size_y, size_z)
    return split[:, 0], split[:, 1]


def turn(values, shift, axis):
    return pltpu.roll(values, shift % values.shape[axis], axis)


def even_cells(shape, step, axis):
    index = lax.broadcasted_iota(jnp.int32, shape, axis)
    return (index & step) == 0


def pair_sum(values, step, axis):
    even = even_cells(values.shape, step, axis)
    return values + jnp.where(even, turn(values, -step, axis), turn(values, step, axis))


def take_even(values, step, axis):
    return jnp.where(even_cells(values.shape, step, axis), values, turn(values, step, axis))


def take_odd(values, step, axis):
    return jnp.where(even_cells(values.shape, step, axis), turn(values, -step, axis), values)


def block_sum(values, step):
    low, high = pair_x(values)
    return pair_sum(pair_sum(low + high, step, 1), step, 2)


def with_diagonal(storage, faces):
    diagonal = storage + faces[0] + faces[1] + faces[2] + faces[3] + faces[4] + faces[5]
    return (storage, faces, diagonal)


def coarsen(operator, step):
    storage, faces, _ = operator
    sides_y = [sum(pair_x(faces[i])) for i in (2, 3)]
    sides_z = [sum(pair_x(faces[i])) for i in (4, 5)]
    new_faces = (
        pair_sum(pair_sum(pair_x(faces[0])[0], step, 1), step, 2),
        pair_sum(pair_sum(pair_x(faces[1])[1], step, 1), step, 2),
        take_even(pair_sum(sides_y[0], step, 2), step, 1),
        take_odd(pair_sum(sides_y[1], step, 2), step, 1),
        take_even(pair_sum(sides_z[0], step, 1), step, 2),
        take_odd(pair_sum(sides_z[1], step, 1), step, 2),
    )
    return with_diagonal(block_sum(storage, step), new_faces)


def enlarge_x(values):
    size_x, size_y, size_z = values.shape
    return jnp.broadcast_to(values[:, None], (size_x, 2, size_y, size_z)).reshape(
        size_x * 2, size_y, size_z
    )


def cycle_kernel(sizes, fac_ref, old_ref, col_ref, out_ref, feat_ref, *scratch):
    levels, (send_sem, recv_sem) = scratch[:-2], scratch[-2:]
    levels = [levels[5 * i : 5 * i + 5] for i in range(4)]
    count_x, count_y = sizes
    at_x, at_y, at_z = (lax.axis_index(axis) for axis in ("gx", "gy", "gz"))
    others = (
        (at_x > 0, {"gx": jnp.maximum(at_x - 1, 0)}),
        (at_x < count_x - 1, {"gx": jnp.minimum(at_x + 1, count_x - 1)}),
        (at_y > 0, {"gy": jnp.maximum(at_y - 1, 0)}),
        (at_y < count_y - 1, {"gy": jnp.minimum(at_y + 1, count_y - 1)}),
    )
    partner = {"gz": 1 - at_z}
    for held, outgoing, beside_x, beside_y, beside_z in levels:
        beside_x[...] = jnp.zeros_like(beside_x)
        beside_y[...] = jnp.zeros_like(beside_y)

    barrier = pltpu.get_barrier_semaphore()
    for there, device in others:

        @pl.when(there)
        def _():
            pl.semaphore_signal(barrier, inc=1, device_id=device, device_id_type=MESH)

    pl.semaphore_signal(barrier, inc=1, device_id=partner, device_id_type=MESH)
    peers = 1 + sum(there.astype(jnp.int32) for there, _ in others)
    pl.semaphore_wait(barrier, peers)

    used = [0, 0, 0, 0]
    turn_of = [0]

    def begin(values, level):
        slot = used[level]
        used[level] += 1
        k = turn_of[0]
        turn_of[0] += 1
        held, outgoing, beside_x, beside_y, beside_z = levels[level]
        size_x, size_y, _ = values.shape
        held[slot] = values
        outgoing[slot, 0] = values[:, :1]
        outgoing[slot, 1] = values[:, size_y - 1 :]
        sources = (
            held.at[slot, pl.ds(0, 1)],
            held.at[slot, pl.ds(size_x - 1, 1)],
            outgoing.at[slot, 0],
            outgoing.at[slot, 1],
        )
        targets = (
            beside_x.at[slot, pl.ds(1, 1)],
            beside_x.at[slot, pl.ds(0, 1)],
            beside_y.at[slot, 1],
            beside_y.at[slot, 0],
        )
        copies = []
        for side, (there, device) in enumerate(others):
            back = side ^ 1
            copy = pltpu.make_async_remote_copy(
                sources[side],
                targets[side],
                send_sem.at[k, side],
                recv_sem.at[k, back],
                device_id=device,
                device_id_type=MESH,
            )
            pl.when(there)(copy.start)
            arrival = pltpu.make_async_remote_copy(
                sources[back],
                targets[back],
                send_sem.at[k, side],
                recv_sem.at[k, side],
                device_id=device,
                device_id_type=MESH,
            )
            copies.append((there, copy, arrival))
        across = pltpu.make_async_remote_copy(
            held.at[slot],
            beside_z.at[slot],
            send_sem.at[k, 4],
            recv_sem.at[k, 4],
            device_id=partner,
            device_id_type=MESH,
        )
        across.start()
        return level, slot, copies, across

    def finish(pending):
        level, slot, copies, across = pending
        for there, copy, arrival in copies:

            @pl.when(there)
            def _():
                copy.wait_send()
                arrival.wait_recv()

        across.wait()
        _, _, beside_x, beside_y, beside_z = levels[level]
        return beside_x[slot], beside_y[slot], beside_z[slot]

    def neighbours(values, beside, step):
        along_x, along_y, along_z = beside
        shape = values.shape
        index_y = lax.broadcasted_iota(jnp.int32, shape, 1)
        index_z = lax.broadcasted_iota(jnp.int32, shape, 2)
        size_y, size_z = shape[1:]
        return (
            jnp.concatenate([along_x[:1], values[:-1]], 0),
            jnp.concatenate([values[1:], along_x[1:]], 0),
            jnp.where(index_y < step, along_y[0], turn(values, step, 1)),
            jnp.where(index_y >= size_y - step, along_y[1], turn(values, -step, 1)),
            turn(jnp.where(index_z >= size_z - step, along_z, values), step, 2),
            turn(jnp.where(index_z < step, along_z, values), -step, 2),
        )

    def apply_with(values, beside, operator, step):
        total = operator[2] * values
        for face, other in zip(operator[1], neighbours(values, beside, step)):
            total = total - face * other
        return total

    def apply_level(values, operator, level):
        return apply_with(values, finish(begin(values, level)), operator, 1 << level)

    def relax(values, rhs, operator, level):
        return values + relax_weight * (rhs - apply_level(values, operator, level)) / operator[2]

    facies = fac_ref[...]
    permeability = table_lookup(facies, PERM_TABLE)
    sent_perm = begin(permeability, 0)
    old = old_ref[...]
    sent_old = begin(old, 0)
    storage = storage_factor * table_lookup(facies, PORE_TABLE)
    source = jnp.broadcast_to(rate_unit * col_ref[...], facies.shape)
    rhs = storage * old + source

    around = list(neighbours(permeability, finish(sent_perm), 1))
    index_z = lax.broadcasted_iota(jnp.int32, facies.shape, 2)
    size_z = facies.shape[2]
    around[4] = jnp.where((index_z == 0) & (at_z == 0), 0.0, around[4])
    around[5] = jnp.where((index_z == size_z - 1) & (at_z == 1), 0.0, around[5])
    faces = [harmonic(permeability, other) for other in around]
    faces[4] = vertical_factor * faces[4]
    faces[5] = vertical_factor * faces[5]
    zero = with_diagonal(storage, faces)
    product = apply_with(old, finish(sent_old), zero, 1)
    state_zero = old + relax_weight * (rhs - product) / zero[2]
    sent_zero = begin(state_zero, 0)
    one = coarsen(zero, 1)
    two = coarsen(one, 2)
    three = coarsen(two, 4)
    scale_three = relax_weight / three[2]
    rhs_one = block_sum(rhs - apply_with(state_zero, finish(sent_zero), zero, 1), 1)
    state_one = relax_weight * rhs_one / one[2]
    rhs_two = block_sum(rhs_one - apply_level(state_one, one, 1), 2)
    state_two = relax_weight * rhs_two / two[2]
    rhs_three = block_sum(rhs_two - apply_level(state_two, two, 2), 4)
    state_three = relax_weight * rhs_three / three[2]
    for _ in range(COARSE_SWEEPS - 1):
        product = apply_level(state_three, three, 3)
        state_three = state_three + scale_three * (rhs_three - product)
    state_two = relax(state_two + enlarge_x(state_three), rhs_two, two, 2)
    state_one = relax(state_one + enlarge_x(state_two), rhs_one, one, 1)
    guess = state_zero + enlarge_x(state_one)
    sent_guess = begin(guess, 0)

    size_x, size_y, _ = facies.shape
    keep_z = (
        lax.broadcasted_iota(jnp.int32, (size_z, size_z // 2), 0)
        == 2 * lax.broadcasted_iota(jnp.int32, (size_z, size_z // 2), 1)
    ).astype(jnp.bfloat16)
    keep_y = (
        2 * lax.broadcasted_iota(jnp.int32, (size_y // 2, size_y), 0)
        == lax.broadcasted_iota(jnp.int32, (size_y // 2, size_y), 1)
    ).astype(jnp.bfloat16)

    def put_mean(channel, field):
        mean = (block_sum(field, 1) * 0.125).astype(jnp.bfloat16)
        for plane in range(size_x // 2):
            rows = jnp.dot(keep_y, mean[plane], preferred_element_type=jnp.float32)
            cells = jnp.dot(
                rows.astype(jnp.bfloat16), keep_z, preferred_element_type=jnp.float32
            )
            feat_ref[channel, plane] = cells

    put_mean(1, table_lookup(facies, LOG_PERM_TABLE))
    put_mean(2, source)
    product = apply_with(guess, finish(sent_guess), zero, 1)
    pressure = guess + relax_weight * (rhs - product) / zero[2]
    out_ref[...] = pressure
    put_mean(0, pressure)


def pressure_cycle(facies, pressure_old, column):
    size_x, size_y, size_z = facies.shape
    counts = (4, 2, 2, COARSE_SWEEPS - 1)
    scratch = []
    for level, count in enumerate(counts):
        planes = size_x >> level
        scratch += [
            pltpu.VMEM((count, planes, size_y, size_z), jnp.float32),
            pltpu.VMEM((count, 2, planes, 1, size_z), jnp.float32),
            pltpu.VMEM((count, 2, size_y, size_z), jnp.float32),
            pltpu.VMEM((count, 2, planes, 1, size_z), jnp.float32),
            pltpu.VMEM((count, planes, size_y, size_z), jnp.float32),
        ]
    turns = sum(counts)
    scratch += [pltpu.SemaphoreType.DMA((turns, 5)), pltpu.SemaphoreType.DMA((turns, 5))]
    return pl.pallas_call(
        functools.partial(cycle_kernel, (lax.axis_size("gx"), lax.axis_size("gy"))),
        out_shape=(
            jax.ShapeDtypeStruct(facies.shape, jnp.float32),
            jax.ShapeDtypeStruct((3, size_x // 2, size_y // 2, size_z // 2), jnp.float32),
        ),
        in_specs=[pl.BlockSpec(memory_space=pltpu.VMEM)] * 3,
        out_specs=[pl.BlockSpec(memory_space=pltpu.VMEM)] * 2,
        scratch_shapes=scratch,
        compiler_params=pltpu.CompilerParams(
            collective_id=0, has_side_effects=True, vmem_limit_bytes=48 * 1024 * 1024
        ),
    )(facies, pressure_old, column)


def well_columns(well_x, well_y, well_rate, start_x, start_y, count_x, count_y):
    along_x = (well_x[:, None] == start_x + jnp.arange(count_x, dtype=jnp.int32)[None, :]).astype(
        jnp.float32
    )
    along_y = (well_y[:, None] == start_y + jnp.arange(count_y, dtype=jnp.int32)[None, :]).astype(
        jnp.float32
    )
    weighted = along_x * well_rate.astype(jnp.float32)[:, None]
    return jnp.dot(weighted.T, along_y, precision=lax.Precision.HIGHEST)


def lanes_of(size_y, size_z):
    return -(-((size_y + 2 * RIM) * (size_z + 2 * RIM)) // 128) * 128


def flat_index(size_y, size_z):
    index = np.arange(lanes_of(size_y, size_z))
    wide = size_z + 2 * RIM
    real = index < wide * (size_y + 2 * RIM)
    row = np.where(real, index // wide - RIM, -100)
    depth = np.where(real, index % wide - RIM, -100)
    return row.astype(np.int32), depth.astype(np.int32)


def own_planes(values):
    channels, size_x, size_y, size_z = values.shape
    lanes = lanes_of(size_y, size_z)
    wide = size_z + 2 * RIM
    padded = jnp.pad(values, ((0, 16 - channels), (0, 0), (0, 0), (0, 2 * RIM)))
    flat = padded.transpose(1, 0, 2, 3).reshape(size_x, 16, size_y * wide)
    start = RIM * wide + RIM
    return jnp.pad(flat, ((0, 0), (0, 0), (start, lanes - start - size_y * wide)))


def conv_matrices(*weights):
    groups = []
    for weight in weights:
        channels = weight.shape[1]
        if channels < 16:
            weight = jnp.pad(weight, ((0, 0), (0, 16 - channels), (0, 0), (0, 0), (0, 0)))
        groups += [weight[:, at : at + 16] for at in range(0, weight.shape[1], 16)]
    stacked = jnp.stack(groups).reshape(len(groups), 16, 16, 3, 9)
    return stacked.transpose(0, 4, 1, 3, 2).reshape(len(groups), 144, 48)


def silu(values):
    return values / (1.0 + jnp.exp(-values))


def network_kernel(
    sizes, blocks, feat_ref, weight_ref, index_ref, pool_index_ref, keep_ref, up_ref, head_ref,
    delta_ref, fields, first, skip, pooled, middle, deep, raised,
    own, own_pool, far, far_pool, rows_in, rows_in_pool, rows_out, rows_out_pool,
    send_sem, recv_sem,
):
    count_x, count_y = sizes
    at_x, at_y, at_z = (lax.axis_index(axis) for axis in ("gx", "gy", "gz"))
    lower = {"gx": jnp.maximum(at_x - 1, 0)}, {"gy": jnp.maximum(at_y - 1, 0)}
    upper = (
        {"gx": jnp.minimum(at_x + 1, count_x - 1)},
        {"gy": jnp.minimum(at_y + 1, count_y - 1)},
    )
    has = ((at_x > 0, at_x < count_x - 1), (at_y > 0, at_y < count_y - 1))
    partner = {"gz": 1 - at_z}
    for ref in (fields, pooled, rows_in, rows_in_pool):
        ref[...] = jnp.zeros_like(ref)

    barrier = pltpu.get_barrier_semaphore()
    for axis in range(2):
        for there, device in ((has[axis][0], lower[axis]), (has[axis][1], upper[axis])):

            @pl.when(there)
            def _():
                pl.semaphore_signal(barrier, inc=1, device_id=device, device_id_type=MESH)

    pl.semaphore_signal(barrier, inc=1, device_id=partner, device_id_type=MESH)
    peers = 1 + sum(there.astype(jnp.int32) for pair in has for there in pair)
    pl.semaphore_wait(barrier, peers)

    def swap(k, axis, to_low, from_low, to_high, from_high):
        low = pltpu.make_async_remote_copy(
            to_low, from_high, send_sem.at[k, 0], recv_sem.at[k, 1],
            device_id=lower[axis], device_id_type=MESH,
        )
        high = pltpu.make_async_remote_copy(
            to_high, from_low, send_sem.at[k, 1], recv_sem.at[k, 0],
            device_id=upper[axis], device_id_type=MESH,
        )
        pl.when(has[axis][0])(low.start)
        pl.when(has[axis][1])(high.start)

        @pl.when(has[axis][0])
        def _():
            low.wait_send()
            high.wait_recv()

        @pl.when(has[axis][1])
        def _():
            high.wait_send()
            low.wait_recv()

    def fill_rims(k, mine, beyond, sent, landed, whole, row, depth, size_y, size_z):
        lanes = mine.shape[2]
        wide = size_z + 2 * RIM
        across = pltpu.make_async_remote_copy(
            mine, beyond, send_sem.at[k, 0], recv_sem.at[k, 0],
            device_id=partner, device_id_type=MESH,
        )
        across.start()
        across.wait()
        planes = mine.shape[0]
        here = (row >= 0) & (row < size_y)
        from_high = here & (depth >= size_z) & (at_z == 0)
        from_low = here & (depth < 0) & (at_z == 1)
        low_at, low_len = low_lanes(size_y, size_z)
        high_at, high_len = high_lanes(size_y, size_z)
        for x in range(planes):
            other = beyond[x].astype(jnp.float32)
            values = mine[x].astype(jnp.float32)
            values = jnp.where(from_high, pltpu.roll(other, size_z, 1), values)
            values = jnp.where(from_low, pltpu.roll(other, lanes - size_z, 1), values)
            values = values.astype(jnp.bfloat16)
            whole[x + RIM] = values
            sent[0, x, :, :low_len] = values[:, low_at : low_at + low_len]
            sent[1, x, :, :high_len] = values[:, high_at : high_at + high_len]
        swap(k + 1, 1, sent.at[0], landed.at[0], sent.at[1], landed.at[1])
        for x in range(planes):
            values = whole[x + RIM].astype(jnp.float32)
            above = jnp.concatenate(
                [landed[0, x].astype(jnp.float32), jnp.zeros((16, lanes - landed.shape[3]), jnp.float32)], 1
            )
            below = jnp.concatenate(
                [landed[1, x].astype(jnp.float32), jnp.zeros((16, lanes - landed.shape[3]), jnp.float32)], 1
            )
            above = pltpu.roll(above, (high_at - size_y * wide) % lanes, 1)
            below = pltpu.roll(below, (low_at + size_y * wide) % lanes, 1)
            values = jnp.where((row < 0) & (row >= -RIM), above, values)
            values = jnp.where(row >= size_y, below, values)
            whole[x + RIM] = values.astype(jnp.bfloat16)
        swap(
            k + 2, 0,
            whole.at[pl.ds(RIM, RIM)], whole.at[pl.ds(0, RIM)],
            whole.at[pl.ds(planes, RIM)], whole.at[pl.ds(planes + RIM, RIM)],
        )

    def on_grid(row, depth, size_y, size_z):
        row, depth = row + at_y * size_y, depth + at_z * size_z
        return (row >= 0) & (row < size_y * count_y) & (depth >= 0) & (depth < 2 * size_z)

    def conv(wide, pieces):
        product = None
        for group, planes in pieces:
            stacked = planes.reshape(48, planes.shape[2])
            term = jnp.dot(weight_ref[group], stacked, preferred_element_type=jnp.float32)
            product = term if product is None else product + term
        lanes = product.shape[1]
        total = None
        for shift in range(9):
            offset = (shift // 3 - 1) * wide + shift % 3 - 1
            part = product[16 * shift : 16 * shift + 16]
            if offset:
                part = pltpu.roll(part, (-offset) % lanes, 1)
            total = part if total is None else total + part
        return silu(total)

    size_x, size_y, size_z = blocks
    pool_x, pool_y, pool_z = (size // 2 for size in blocks)
    wide, wide_pool = size_z + 2 * RIM, pool_z + 2 * RIM
    row, depth = index_ref[0:1], index_ref[1:2]
    row_pool, depth_pool = pool_index_ref[0:1], pool_index_ref[1:2]
    grid = on_grid(row, depth, size_y, size_z)
    grid_pool = on_grid(row_pool, depth_pool, pool_y, pool_z)

    def masked(values, mask, plane, size):
        plane = plane + at_x * size
        inside = jnp.where((plane >= 0) & (plane < size * count_x), 1.0, 0.0)
        return (jnp.where(mask, values, 0.0) * inside).astype(jnp.bfloat16)

    own[...] = feat_ref[...]
    fill_rims(0, own, far, rows_out, rows_in, fields, row, depth, size_y, size_z)

    @pl.loop(0, size_x + 4, unroll=2)
    def _(x):
        first[x] = masked(conv(wide, [(0, fields[pl.ds(x, 3)])]), grid, x - 2, size_x)

    @pl.loop(0, size_x + 2, unroll=2)
    def _(x):
        skip[x] = masked(conv(wide, [(1, first[pl.ds(x, 3)])]), grid, x - 1, size_x)

    @pl.loop(0, pool_x, unroll=2)
    def _(x):
        total = skip[2 * x + 1].astype(jnp.float32) + skip[2 * x + 2].astype(jnp.float32)
        lanes = total.shape[1]
        total = total + pltpu.roll(total, lanes - 1, 1)
        total = total + pltpu.roll(total, lanes - wide, 1)
        mean = (total * 0.125).astype(jnp.bfloat16)
        own_pool[x] = jnp.dot(mean, keep_ref[...], preferred_element_type=jnp.float32).astype(
            jnp.bfloat16
        )

    fill_rims(
        3, own_pool, far_pool, rows_out_pool, rows_in_pool, pooled, row_pool, depth_pool,
        pool_y, pool_z,
    )

    @pl.loop(0, pool_x + 4, unroll=2)
    def _(x):
        middle[x] = masked(conv(wide_pool, [(2, pooled[pl.ds(x, 3)])]), grid_pool, x - 2, pool_x)

    @pl.loop(0, pool_x + 2, unroll=2)
    def _(x):
        values = masked(conv(wide_pool, [(3, middle[pl.ds(x, 3)])]), grid_pool, x - 1, pool_x)
        deep[x] = jnp.dot(values, up_ref[...], preferred_element_type=jnp.float32).astype(
            jnp.bfloat16
        )

    for x in range(size_x + 2):
        raised[x] = deep[(x + 1) // 2]

    @pl.loop(0, size_x, unroll=2)
    def _(x):
        values = conv(wide, [(4, skip[pl.ds(x, 3)]), (5, raised[pl.ds(x, 3)])])
        values = values.astype(jnp.bfloat16).astype(jnp.float32)
        delta_ref[x] = jnp.sum(values * head_ref[...], axis=0, keepdims=True)


def low_lanes(size_y, size_z):
    wide = size_z + 2 * RIM
    start = RIM * wide // 128 * 128
    return start, -(-(2 * RIM * wide) // 128) * 128 - start


def high_lanes(size_y, size_z):
    wide = size_z + 2 * RIM
    start = size_y * wide // 128 * 128
    return start, -(-((size_y + RIM) * wide) // 128) * 128 - start


def network(features, weights, head, blocks):
    pools = tuple(size // 2 for size in blocks)
    lanes, lanes_pool = lanes_of(*blocks[1:]), lanes_of(*pools[1:])
    edge, edge_pool = (
        max(low_lanes(*s[1:])[1], high_lanes(*s[1:])[1]) for s in (blocks, pools)
    )
    row, depth = flat_index(*blocks[1:])
    row_pool, depth_pool = flat_index(*pools[1:])
    owned = (row_pool >= 0) & (row_pool < pools[1]) & (depth_pool >= 0) & (depth_pool < pools[2])
    keep = (row[:, None] == 2 * row_pool[None]) & (depth[:, None] == 2 * depth_pool[None])
    keep = (keep & owned[None]).astype(ml_dtypes.bfloat16)
    up = (row_pool[:, None] == (row // 2)[None]) & (depth_pool[:, None] == (depth // 2)[None])
    up = (up & (row_pool > -100)[:, None]).astype(ml_dtypes.bfloat16)
    whole = pl.BlockSpec(memory_space=pltpu.VMEM)
    x, px, half = blocks[0], pools[0], jnp.bfloat16
    return pl.pallas_call(
        functools.partial(network_kernel, (lax.axis_size("gx"), lax.axis_size("gy")), blocks),
        out_shape=jax.ShapeDtypeStruct((x, 1, lanes), jnp.float32),
        in_specs=[whole] * 7,
        out_specs=whole,
        scratch_shapes=[
            pltpu.VMEM((x + 2 * RIM, 16, lanes), half),
            pltpu.VMEM((x + 4, 16, lanes), half),
            pltpu.VMEM((x + 2, 16, lanes), half),
            pltpu.VMEM((px + 2 * RIM, 16, lanes_pool), half),
            pltpu.VMEM((px + 4, 16, lanes_pool), half),
            pltpu.VMEM((px + 2, 16, lanes), half),
            pltpu.VMEM((x + 2, 16, lanes), half),
            pltpu.VMEM((x, 16, lanes), half),
            pltpu.VMEM((px, 16, lanes_pool), half),
            pltpu.VMEM((x, 16, lanes), half),
            pltpu.VMEM((px, 16, lanes_pool), half),
            pltpu.VMEM((2, x, 16, edge), half),
            pltpu.VMEM((2, px, 16, edge_pool), half),
            pltpu.VMEM((2, x, 16, edge), half),
            pltpu.VMEM((2, px, 16, edge_pool), half),
            pltpu.SemaphoreType.DMA((6, 2)),
            pltpu.SemaphoreType.DMA((6, 2)),
        ],
        compiler_params=pltpu.CompilerParams(
            collective_id=1, has_side_effects=True, vmem_limit_bytes=48 * 1024 * 1024
        ),
    )(
        features, weights, jnp.asarray(np.stack([row, depth])),
        jnp.asarray(np.stack([row_pool, depth_pool])), jnp.asarray(keep), jnp.asarray(up), head,
    )


def on_device(
    facies, pressure_old, saturation, well_x, well_y, well_rate,
    enc_first, enc_second, mid_first, mid_second, dec_weight, head_weight,
):
    size_x, size_y, size_z = facies.shape
    column = well_columns(
        well_x, well_y, well_rate,
        lax.axis_index("gx") * size_x, lax.axis_index("gy") * size_y, size_x, size_y,
    )
    pressure, means = pressure_cycle(facies, pressure_old, column[:, :, None])
    blocks = saturation.shape
    wide = blocks[2] + 2 * RIM
    features = jnp.concatenate([saturation[None], means], 0).astype(jnp.bfloat16)
    weights = conv_matrices(enc_first, enc_second, mid_first, mid_second, dec_weight)
    delta = network(
        own_planes(features), weights, head_weight.astype(jnp.float32)[:, None], blocks
    )
    delta = delta[:, 0, RIM * wide + RIM : RIM * wide + RIM + blocks[1] * wide]
    delta = delta.reshape(blocks[0], blocks[1], wide)[:, :, : blocks[2]]
    return (pressure, saturation + delta)


def solution(mesh):
    return jax.shard_map(
        on_device,
        mesh=mesh,
        in_specs=(P(("run", "gx"), "gy", "gz"),) * 3 + (P("run"),) * 3 + (P(),) * 6,
        out_specs=(P(("run", "gx"), "gy", "gz"), P(("run", "gx"), "gy", "gz")),
        check_vma=False,
    )
```

```python
import functools

import jax
import jax.numpy as jnp
import ml_dtypes
import numpy as np
from jax import lax
from jax.experimental import pallas as pl
from jax.experimental.pallas import tpu as pltpu
from jax.sharding import PartitionSpec as P

COARSE_SWEEPS = 8
PERM_TABLE = (0.02, 0.15, 0.8, 2.5, 9.0)
LOG_PERM_TABLE = (-3.912023, -1.89712, -0.223144, 0.916291, 2.197225)
PORE_TABLE = (0.05, 0.12, 0.2, 0.25, 0.3)
storage_factor = 0.0002
vertical_factor = 0.5
relax_weight = 0.6666667
rate_unit = 0.05
MESH = pl.DeviceIdType.MESH
RIM = 3


def table_lookup(facies, table):
    result = jnp.full(facies.shape, table[0], jnp.float32)
    for entry_index in range(1, len(table)):
        result = jnp.where(facies == entry_index, jnp.float32(table[entry_index]), result)
    return result


def harmonic(lower, upper):
    return 2.0 * lower * upper / (lower + upper)


def pair_x(values):
    size_x, size_y, size_z = values.shape
    split = values.reshape(size_x // 2, 2, size_y, size_z)
    return split[:, 0], split[:, 1]


def turn(values, shift, axis):
    return pltpu.roll(values, shift % values.shape[axis], axis)


def even_cells(shape, step, axis):
    index = lax.broadcasted_iota(jnp.int32, shape, axis)
    return (index & step) == 0


def pair_sum(values, step, axis):
    even = even_cells(values.shape, step, axis)
    return values + jnp.where(even, turn(values, -step, axis), turn(values, step, axis))


def take_even(values, step, axis):
    return jnp.where(even_cells(values.shape, step, axis), values, turn(values, step, axis))


def take_odd(values, step, axis):
    return jnp.where(even_cells(values.shape, step, axis), turn(values, -step, axis), values)


def block_sum(values, step):
    low, high = pair_x(values)
    return pair_sum(pair_sum(low + high, step, 1), step, 2)


def with_diagonal(storage, faces):
    diagonal = storage + faces[0] + faces[1] + faces[2] + faces[3] + faces[4] + faces[5]
    return (storage, faces, diagonal)


def coarsen(operator, step):
    storage, faces, _ = operator
    sides_y = [sum(pair_x(faces[i])) for i in (2, 3)]
    sides_z = [sum(pair_x(faces[i])) for i in (4, 5)]
    new_faces = (
        pair_sum(pair_sum(pair_x(faces[0])[0], step, 1), step, 2),
        pair_sum(pair_sum(pair_x(faces[1])[1], step, 1), step, 2),
        take_even(pair_sum(sides_y[0], step, 2), step, 1),
        take_odd(pair_sum(sides_y[1], step, 2), step, 1),
        take_even(pair_sum(sides_z[0], step, 1), step, 2),
        take_odd(pair_sum(sides_z[1], step, 1), step, 2),
    )
    return with_diagonal(block_sum(storage, step), new_faces)


def enlarge_x(values):
    size_x, size_y, size_z = values.shape
    return jnp.broadcast_to(values[:, None], (size_x, 2, size_y, size_z)).reshape(
        size_x * 2, size_y, size_z
    )


def cycle_kernel(sizes, fac_ref, old_ref, col_ref, out_ref, feat_ref, *scratch):
    levels, (send_sem, recv_sem) = scratch[:-2], scratch[-2:]
    levels = [levels[5 * i : 5 * i + 5] for i in range(4)]
    count_x, count_y = sizes
    at_x, at_y, at_z = (lax.axis_index(axis) for axis in ("gx", "gy", "gz"))
    others = (
        (at_x > 0, {"gx": jnp.maximum(at_x - 1, 0)}),
        (at_x < count_x - 1, {"gx": jnp.minimum(at_x + 1, count_x - 1)}),
        (at_y > 0, {"gy": jnp.maximum(at_y - 1, 0)}),
        (at_y < count_y - 1, {"gy": jnp.minimum(at_y + 1, count_y - 1)}),
    )
    partner = {"gz": 1 - at_z}
    for held, outgoing, beside_x, beside_y, beside_z in levels:
        beside_x[...] = jnp.zeros_like(beside_x)
        beside_y[...] = jnp.zeros_like(beside_y)

    barrier = pltpu.get_barrier_semaphore()
    for there, device in others:

        @pl.when(there)
        def _():
            pl.semaphore_signal(barrier, inc=1, device_id=device, device_id_type=MESH)

    pl.semaphore_signal(barrier, inc=1, device_id=partner, device_id_type=MESH)
    peers = 1 + sum(there.astype(jnp.int32) for there, _ in others)
    pl.semaphore_wait(barrier, peers)

    used = [0, 0, 0, 0]
    turn_of = [0]

    def begin(values, level):
        slot = used[level]
        used[level] += 1
        k = turn_of[0]
        turn_of[0] += 1
        held, outgoing, beside_x, beside_y, beside_z = levels[level]
        size_x, size_y, _ = values.shape
        held[slot] = values
        outgoing[slot, 0] = values[:, :1]
        outgoing[slot, 1] = values[:, size_y - 1 :]
        sources = (
            held.at[slot, pl.ds(0, 1)],
            held.at[slot, pl.ds(size_x - 1, 1)],
            outgoing.at[slot, 0],
            outgoing.at[slot, 1],
        )
        targets = (
            beside_x.at[slot, pl.ds(1, 1)],
            beside_x.at[slot, pl.ds(0, 1)],
            beside_y.at[slot, 1],
            beside_y.at[slot, 0],
        )
        copies = []
        for side, (there, device) in enumerate(others):
            back = side ^ 1
            copy = pltpu.make_async_remote_copy(
                sources[side],
                targets[side],
                send_sem.at[k, side],
                recv_sem.at[k, back],
                device_id=device,
                device_id_type=MESH,
            )
            pl.when(there)(copy.start)
            arrival = pltpu.make_async_remote_copy(
                sources[back],
                targets[back],
                send_sem.at[k, side],
                recv_sem.at[k, side],
                device_id=device,
                device_id_type=MESH,
            )
            copies.append((there, copy, arrival))
        across = pltpu.make_async_remote_copy(
            held.at[slot],
            beside_z.at[slot],
            send_sem.at[k, 4],
            recv_sem.at[k, 4],
            device_id=partner,
            device_id_type=MESH,
        )
        across.start()
        return level, slot, copies, across

    def finish(pending):
        level, slot, copies, across = pending
        for there, copy, arrival in copies:

            @pl.when(there)
            def _():
                copy.wait_send()
                arrival.wait_recv()

        across.wait()
        _, _, beside_x, beside_y, beside_z = levels[level]
        return beside_x[slot], beside_y[slot], beside_z[slot]

    def neighbours(values, beside, step):
        along_x, along_y, along_z = beside
        shape = values.shape
        index_y = lax.broadcasted_iota(jnp.int32, shape, 1)
        index_z = lax.broadcasted_iota(jnp.int32, shape, 2)
        size_y, size_z = shape[1:]
        return (
            jnp.concatenate([along_x[:1], values[:-1]], 0),
            jnp.concatenate([values[1:], along_x[1:]], 0),
            jnp.where(index_y < step, along_y[0], turn(values, step, 1)),
            jnp.where(index_y >= size_y - step, along_y[1], turn(values, -step, 1)),
            turn(jnp.where(index_z >= size_z - step, along_z, values), step, 2),
            turn(jnp.where(index_z < step, along_z, values), -step, 2),
        )

    def apply_with(values, beside, operator, step):
        total = operator[2] * values
        for face, other in zip(operator[1], neighbours(values, beside, step)):
            total = total - face * other
        return total

    def apply_level(values, operator, level):
        return apply_with(values, finish(begin(values, level)), operator, 1 << level)

    def relax(values, rhs, operator, level):
        return values + relax_weight * (rhs - apply_level(values, operator, level)) / operator[2]

    facies = fac_ref[...]
    permeability = table_lookup(facies, PERM_TABLE)
    sent_perm = begin(permeability, 0)
    old = old_ref[...]
    sent_old = begin(old, 0)
    storage = storage_factor * table_lookup(facies, PORE_TABLE)
    source = jnp.broadcast_to(rate_unit * col_ref[...], facies.shape)
    rhs = storage * old + source

    around = list(neighbours(permeability, finish(sent_perm), 1))
    index_z = lax.broadcasted_iota(jnp.int32, facies.shape, 2)
    size_z = facies.shape[2]
    around[4] = jnp.where((index_z == 0) & (at_z == 0), 0.0, around[4])
    around[5] = jnp.where((index_z == size_z - 1) & (at_z == 1), 0.0, around[5])
    faces = [harmonic(permeability, other) for other in around]
    faces[4] = vertical_factor * faces[4]
    faces[5] = vertical_factor * faces[5]
    zero = with_diagonal(storage, faces)
    product = apply_with(old, finish(sent_old), zero, 1)
    state_zero = old + relax_weight * (rhs - product) / zero[2]
    sent_zero = begin(state_zero, 0)
    one = coarsen(zero, 1)
    two = coarsen(one, 2)
    three = coarsen(two, 4)
    scale_three = relax_weight / three[2]
    rhs_one = block_sum(rhs - apply_with(state_zero, finish(sent_zero), zero, 1), 1)
    state_one = relax_weight * rhs_one / one[2]
    rhs_two = block_sum(rhs_one - apply_level(state_one, one, 1), 2)
    state_two = relax_weight * rhs_two / two[2]
    rhs_three = block_sum(rhs_two - apply_level(state_two, two, 2), 4)
    state_three = relax_weight * rhs_three / three[2]
    for _ in range(COARSE_SWEEPS - 1):
        product = apply_level(state_three, three, 3)
        state_three = state_three + scale_three * (rhs_three - product)
    state_two = relax(state_two + enlarge_x(state_three), rhs_two, two, 2)
    state_one = relax(state_one + enlarge_x(state_two), rhs_one, one, 1)
    guess = state_zero + enlarge_x(state_one)
    sent_guess = begin(guess, 0)

    size_x, size_y, _ = facies.shape
    keep_z = (
        lax.broadcasted_iota(jnp.int32, (size_z, size_z // 2), 0)
        == 2 * lax.broadcasted_iota(jnp.int32, (size_z, size_z // 2), 1)
    ).astype(jnp.bfloat16)
    keep_y = (
        2 * lax.broadcasted_iota(jnp.int32, (size_y // 2, size_y), 0)
        == lax.broadcasted_iota(jnp.int32, (size_y // 2, size_y), 1)
    ).astype(jnp.bfloat16)

    def put_mean(channel, field):
        mean = (block_sum(field, 1) * 0.125).astype(jnp.bfloat16)
        for plane in range(size_x // 2):
            rows = jnp.dot(keep_y, mean[plane], preferred_element_type=jnp.float32)
            cells = jnp.dot(
                rows.astype(jnp.bfloat16), keep_z, preferred_element_type=jnp.float32
            )
            feat_ref[channel, plane] = cells

    put_mean(1, table_lookup(facies, LOG_PERM_TABLE))
    put_mean(2, source)
    product = apply_with(guess, finish(sent_guess), zero, 1)
    pressure = guess + relax_weight * (rhs - product) / zero[2]
    out_ref[...] = pressure
    put_mean(0, pressure)


def pressure_cycle(facies, pressure_old, column):
    size_x, size_y, size_z = facies.shape
    counts = (4, 2, 2, COARSE_SWEEPS - 1)
    scratch = []
    for level, count in enumerate(counts):
        planes = size_x >> level
        scratch += [
            pltpu.VMEM((count, planes, size_y, size_z), jnp.float32),
            pltpu.VMEM((count, 2, planes, 1, size_z), jnp.float32),
            pltpu.VMEM((count, 2, size_y, size_z), jnp.float32),
            pltpu.VMEM((count, 2, planes, 1, size_z), jnp.float32),
            pltpu.VMEM((count, planes, size_y, size_z), jnp.float32),
        ]
    turns = sum(counts)
    scratch += [pltpu.SemaphoreType.DMA((turns, 5)), pltpu.SemaphoreType.DMA((turns, 5))]
    return pl.pallas_call(
        functools.partial(cycle_kernel, (lax.axis_size("gx"), lax.axis_size("gy"))),
        out_shape=(
            jax.ShapeDtypeStruct(facies.shape, jnp.float32),
            jax.ShapeDtypeStruct((3, size_x // 2, size_y // 2, size_z // 2), jnp.float32),
        ),
        in_specs=[pl.BlockSpec(memory_space=pltpu.VMEM)] * 3,
        out_specs=[pl.BlockSpec(memory_space=pltpu.VMEM)] * 2,
        scratch_shapes=scratch,
        compiler_params=pltpu.CompilerParams(
            collective_id=0, has_side_effects=True, vmem_limit_bytes=48 * 1024 * 1024
        ),
    )(facies, pressure_old, column)


def well_columns(well_x, well_y, well_rate, start_x, start_y, count_x, count_y):
    along_x = (well_x[:, None] == start_x + jnp.arange(count_x, dtype=jnp.int32)[None, :]).astype(
        jnp.float32
    )
    along_y = (well_y[:, None] == start_y + jnp.arange(count_y, dtype=jnp.int32)[None, :]).astype(
        jnp.float32
    )
    weighted = along_x * well_rate.astype(jnp.float32)[:, None]
    return jnp.dot(weighted.T, along_y, precision=lax.Precision.HIGHEST)


def lanes_of(size_y, size_z):
    return -(-((size_y + 2 * RIM) * (size_z + 2 * RIM)) // 128) * 128


def flat_index(size_y, size_z):
    index = np.arange(lanes_of(size_y, size_z))
    wide = size_z + 2 * RIM
    real = index < wide * (size_y + 2 * RIM)
    row = np.where(real, index // wide - RIM, -100)
    depth = np.where(real, index % wide - RIM, -100)
    return row.astype(np.int32), depth.astype(np.int32)


def own_planes(values):
    channels, size_x, size_y, size_z = values.shape
    lanes = lanes_of(size_y, size_z)
    wide = size_z + 2 * RIM
    padded = jnp.pad(values, ((0, 16 - channels), (0, 0), (0, 0), (0, 2 * RIM)))
    flat = padded.transpose(1, 0, 2, 3).reshape(size_x, 16, size_y * wide)
    start = RIM * wide + RIM
    return jnp.pad(flat, ((0, 0), (0, 0), (start, lanes - start - size_y * wide)))


def conv_matrices(*weights):
    groups = []
    for weight in weights:
        channels = weight.shape[1]
        if channels < 16:
            weight = jnp.pad(weight, ((0, 0), (0, 16 - channels), (0, 0), (0, 0), (0, 0)))
        groups += [weight[:, at : at + 16] for at in range(0, weight.shape[1], 16)]
    stacked = jnp.stack(groups).reshape(len(groups), 16, 16, 3, 9)
    return stacked.transpose(0, 4, 1, 3, 2).reshape(len(groups), 144, 48)


def silu(values):
    return values / (1.0 + jnp.exp(-values))


def network_kernel(
    sizes, blocks, feat_ref, weight_ref, index_ref, pool_index_ref, keep_ref, up_ref, head_ref,
    delta_ref, fields, first, skip, pooled, middle, deep, raised,
    own, own_pool, far, far_pool, rows_in, rows_in_pool, rows_out, rows_out_pool,
    send_sem, recv_sem,
):
    count_x, count_y = sizes
    at_x, at_y, at_z = (lax.axis_index(axis) for axis in ("gx", "gy", "gz"))
    lower = {"gx": jnp.maximum(at_x - 1, 0)}, {"gy": jnp.maximum(at_y - 1, 0)}
    upper = (
        {"gx": jnp.minimum(at_x + 1, count_x - 1)},
        {"gy": jnp.minimum(at_y + 1, count_y - 1)},
    )
    has = ((at_x > 0, at_x < count_x - 1), (at_y > 0, at_y < count_y - 1))
    partner = {"gz": 1 - at_z}
    for ref in (fields, pooled, rows_in, rows_in_pool):
        ref[...] = jnp.zeros_like(ref)

    barrier = pltpu.get_barrier_semaphore()
    for axis in range(2):
        for there, device in ((has[axis][0], lower[axis]), (has[axis][1], upper[axis])):

            @pl.when(there)
            def _():
                pl.semaphore_signal(barrier, inc=1, device_id=device, device_id_type=MESH)

    pl.semaphore_signal(barrier, inc=1, device_id=partner, device_id_type=MESH)
    peers = 1 + sum(there.astype(jnp.int32) for pair in has for there in pair)
    pl.semaphore_wait(barrier, peers)

    def swap(k, axis, to_low, from_low, to_high, from_high):
        low = pltpu.make_async_remote_copy(
            to_low, from_high, send_sem.at[k, 0], recv_sem.at[k, 1],
            device_id=lower[axis], device_id_type=MESH,
        )
        high = pltpu.make_async_remote_copy(
            to_high, from_low, send_sem.at[k, 1], recv_sem.at[k, 0],
            device_id=upper[axis], device_id_type=MESH,
        )
        pl.when(has[axis][0])(low.start)
        pl.when(has[axis][1])(high.start)

        @pl.when(has[axis][0])
        def _():
            low.wait_send()
            high.wait_recv()

        @pl.when(has[axis][1])
        def _():
            high.wait_send()
            low.wait_recv()

    def fill_rims(k, mine, beyond, sent, landed, whole, row, depth, size_y, size_z):
        lanes = mine.shape[2]
        wide = size_z + 2 * RIM
        across = pltpu.make_async_remote_copy(
            mine, beyond, send_sem.at[k, 0], recv_sem.at[k, 0],
            device_id=partner, device_id_type=MESH,
        )
        across.start()
        across.wait()
        planes = mine.shape[0]
        here = (row >= 0) & (row < size_y)
        from_high = here & (depth >= size_z) & (at_z == 0)
        from_low = here & (depth < 0) & (at_z == 1)
        low_at, low_len = low_lanes(size_y, size_z)
        high_at, high_len = high_lanes(size_y, size_z)
        for x in range(planes):
            other = beyond[x].astype(jnp.float32)
            values = mine[x].astype(jnp.float32)
            values = jnp.where(from_high, pltpu.roll(other, size_z, 1), values)
            values = jnp.where(from_low, pltpu.roll(other, lanes - size_z, 1), values)
            values = values.astype(jnp.bfloat16)
            whole[x + RIM] = values
            sent[0, x, :, :low_len] = values[:, low_at : low_at + low_len]
            sent[1, x, :, :high_len] = values[:, high_at : high_at + high_len]
        swap(k + 1, 1, sent.at[0], landed.at[0], sent.at[1], landed.at[1])
        for x in range(planes):
            values = whole[x + RIM].astype(jnp.float32)
            above = jnp.concatenate(
                [landed[0, x].astype(jnp.float32), jnp.zeros((16, lanes - landed.shape[3]), jnp.float32)], 1
            )
            below = jnp.concatenate(
                [landed[1, x].astype(jnp.float32), jnp.zeros((16, lanes - landed.shape[3]), jnp.float32)], 1
            )
            above = pltpu.roll(above, (high_at - size_y * wide) % lanes, 1)
            below = pltpu.roll(below, (low_at + size_y * wide) % lanes, 1)
            values = jnp.where((row < 0) & (row >= -RIM), above, values)
            values = jnp.where(row >= size_y, below, values)
            whole[x + RIM] = values.astype(jnp.bfloat16)
        swap(
            k + 2, 0,
            whole.at[pl.ds(RIM, RIM)], whole.at[pl.ds(0, RIM)],
            whole.at[pl.ds(planes, RIM)], whole.at[pl.ds(planes + RIM, RIM)],
        )

    def on_grid(row, depth, size_y, size_z):
        row, depth = row + at_y * size_y, depth + at_z * size_z
        return (row >= 0) & (row < size_y * count_y) & (depth >= 0) & (depth < 2 * size_z)

    def conv(wide, pieces):
        product = None
        for group, planes in pieces:
            stacked = planes.reshape(48, planes.shape[2])
            term = jnp.dot(weight_ref[group], stacked, preferred_element_type=jnp.float32)
            product = term if product is None else product + term
        lanes = product.shape[1]
        total = None
        for shift in range(9):
            offset = (shift // 3 - 1) * wide + shift % 3 - 1
            part = product[16 * shift : 16 * shift + 16]
            if offset:
                part = pltpu.roll(part, (-offset) % lanes, 1)
            total = part if total is None else total + part
        return silu(total)

    size_x, size_y, size_z = blocks
    pool_x, pool_y, pool_z = (size // 2 for size in blocks)
    wide, wide_pool = size_z + 2 * RIM, pool_z + 2 * RIM
    row, depth = index_ref[0:1], index_ref[1:2]
    row_pool, depth_pool = pool_index_ref[0:1], pool_index_ref[1:2]
    grid = on_grid(row, depth, size_y, size_z)
    grid_pool = on_grid(row_pool, depth_pool, pool_y, pool_z)

    def masked(values, mask, plane, size):
        plane = plane + at_x * size
        inside = jnp.where((plane >= 0) & (plane < size * count_x), 1.0, 0.0)
        return (jnp.where(mask, values, 0.0) * inside).astype(jnp.bfloat16)

    own[...] = feat_ref[...]
    fill_rims(0, own, far, rows_out, rows_in, fields, row, depth, size_y, size_z)

    @pl.loop(0, size_x + 4, unroll=4)
    def _(x):
        first[x] = masked(conv(wide, [(0, fields[pl.ds(x, 3)])]), grid, x - 2, size_x)

    @pl.loop(0, size_x + 2, unroll=5)
    def _(x):
        skip[x] = masked(conv(wide, [(1, first[pl.ds(x, 3)])]), grid, x - 1, size_x)

    @pl.loop(0, pool_x, unroll=2)
    def _(x):
        total = skip[2 * x + 1].astype(jnp.float32) + skip[2 * x + 2].astype(jnp.float32)
        lanes = total.shape[1]
        total = total + pltpu.roll(total, lanes - 1, 1)
        total = total + pltpu.roll(total, lanes - wide, 1)
        mean = (total * 0.125).astype(jnp.bfloat16)
        own_pool[x] = jnp.dot(mean, keep_ref[...], preferred_element_type=jnp.float32).astype(
            jnp.bfloat16
        )

    fill_rims(
        3, own_pool, far_pool, rows_out_pool, rows_in_pool, pooled, row_pool, depth_pool,
        pool_y, pool_z,
    )

    @pl.loop(0, pool_x + 4, unroll=2)
    def _(x):
        middle[x] = masked(conv(wide_pool, [(2, pooled[pl.ds(x, 3)])]), grid_pool, x - 2, pool_x)

    @pl.loop(0, pool_x + 2, unroll=2)
    def _(x):
        values = masked(conv(wide_pool, [(3, middle[pl.ds(x, 3)])]), grid_pool, x - 1, pool_x)
        deep[x] = jnp.dot(values, up_ref[...], preferred_element_type=jnp.float32).astype(
            jnp.bfloat16
        )

    for x in range(size_x + 2):
        raised[x] = deep[(x + 1) // 2]

    @pl.loop(0, size_x, unroll=4)
    def _(x):
        values = conv(wide, [(4, skip[pl.ds(x, 3)]), (5, raised[pl.ds(x, 3)])])
        values = values.astype(jnp.bfloat16).astype(jnp.float32)
        delta_ref[x] = jnp.sum(values * head_ref[...], axis=0, keepdims=True)


def low_lanes(size_y, size_z):
    wide = size_z + 2 * RIM
    start = RIM * wide // 128 * 128
    return start, -(-(2 * RIM * wide) // 128) * 128 - start


def high_lanes(size_y, size_z):
    wide = size_z + 2 * RIM
    start = size_y * wide // 128 * 128
    return start, -(-((size_y + RIM) * wide) // 128) * 128 - start


def network(features, weights, head, blocks):
    pools = tuple(size // 2 for size in blocks)
    lanes, lanes_pool = lanes_of(*blocks[1:]), lanes_of(*pools[1:])
    edge, edge_pool = (
        max(low_lanes(*s[1:])[1], high_lanes(*s[1:])[1]) for s in (blocks, pools)
    )
    row, depth = flat_index(*blocks[1:])
    row_pool, depth_pool = flat_index(*pools[1:])
    owned = (row_pool >= 0) & (row_pool < pools[1]) & (depth_pool >= 0) & (depth_pool < pools[2])
    keep = (row[:, None] == 2 * row_pool[None]) & (depth[:, None] == 2 * depth_pool[None])
    keep = (keep & owned[None]).astype(ml_dtypes.bfloat16)
    up = (row_pool[:, None] == (row // 2)[None]) & (depth_pool[:, None] == (depth // 2)[None])
    up = (up & (row_pool > -100)[:, None]).astype(ml_dtypes.bfloat16)
    whole = pl.BlockSpec(memory_space=pltpu.VMEM)
    x, px, half = blocks[0], pools[0], jnp.bfloat16
    return pl.pallas_call(
        functools.partial(network_kernel, (lax.axis_size("gx"), lax.axis_size("gy")), blocks),
        out_shape=jax.ShapeDtypeStruct((x, 1, lanes), jnp.float32),
        in_specs=[whole] * 7,
        out_specs=whole,
        scratch_shapes=[
            pltpu.VMEM((x + 2 * RIM, 16, lanes), half),
            pltpu.VMEM((x + 4, 16, lanes), half),
            pltpu.VMEM((x + 2, 16, lanes), half),
            pltpu.VMEM((px + 2 * RIM, 16, lanes_pool), half),
            pltpu.VMEM((px + 4, 16, lanes_pool), half),
            pltpu.VMEM((px + 2, 16, lanes), half),
            pltpu.VMEM((x + 2, 16, lanes), half),
            pltpu.VMEM((x, 16, lanes), half),
            pltpu.VMEM((px, 16, lanes_pool), half),
            pltpu.VMEM((x, 16, lanes), half),
            pltpu.VMEM((px, 16, lanes_pool), half),
            pltpu.VMEM((2, x, 16, edge), half),
            pltpu.VMEM((2, px, 16, edge_pool), half),
            pltpu.VMEM((2, x, 16, edge), half),
            pltpu.VMEM((2, px, 16, edge_pool), half),
            pltpu.SemaphoreType.DMA((6, 2)),
            pltpu.SemaphoreType.DMA((6, 2)),
        ],
        compiler_params=pltpu.CompilerParams(
            collective_id=1, has_side_effects=True, vmem_limit_bytes=48 * 1024 * 1024
        ),
    )(
        features, weights, jnp.asarray(np.stack([row, depth])),
        jnp.asarray(np.stack([row_pool, depth_pool])), jnp.asarray(keep), jnp.asarray(up), head,
    )


def on_device(
    facies, pressure_old, saturation, well_x, well_y, well_rate,
    enc_first, enc_second, mid_first, mid_second, dec_weight, head_weight,
):
    size_x, size_y, size_z = facies.shape
    column = well_columns(
        well_x, well_y, well_rate,
        lax.axis_index("gx") * size_x, lax.axis_index("gy") * size_y, size_x, size_y,
    )
    pressure, means = pressure_cycle(facies, pressure_old, column[:, :, None])
    blocks = saturation.shape
    wide = blocks[2] + 2 * RIM
    features = jnp.concatenate([saturation[None], means], 0).astype(jnp.bfloat16)
    weights = conv_matrices(enc_first, enc_second, mid_first, mid_second, dec_weight)
    delta = network(
        own_planes(features), weights, head_weight.astype(jnp.float32)[:, None], blocks
    )
    delta = delta[:, 0, RIM * wide + RIM : RIM * wide + RIM + blocks[1] * wide]
    delta = delta.reshape(blocks[0], blocks[1], wide)[:, :, : blocks[2]]
    return (pressure, saturation + delta)


def solution(mesh):
    return jax.shard_map(
        on_device,
        mesh=mesh,
        in_specs=(P(("run", "gx"), "gy", "gz"),) * 3 + (P("run"),) * 3 + (P(),) * 6,
        out_specs=(P(("run", "gx"), "gy", "gz"), P(("run", "gx"), "gy", "gz")),
        check_vma=False,
    )
```
